512 devices in a mesh: grp: 8 (over y, core), leaf: 64 (over x, z).
Axes of the slice: x: 4, y: 4, z: 16, core: 2. Of those that a mesh axis runs over, the one named last changes fastest.
Arguments:
- vectors: float32 [16, 524288], P(None, ('grp', 'leaf')), may hold values from -6 to 6
- points: float32 [3, 524288], P(None, ('grp', 'leaf')), may hold values from -1 to 2
- near_lists: int32 [1024, 6], P(('grp', 'leaf')), may hold values from -1 to 5, as said below
- inter_lists: int32 [1024, 16], P(('grp', 'leaf')), may hold values from 0 to 127, as said below
- skeleton: int32 [1024, 64], P(('grp', 'leaf')), may hold values from 0 to 511, as said below
- interp: float32 [1024, 64, 512], P(('grp', 'leaf')), may hold values from -0.25 to 0.25
- transfer: float32 [1024, 64, 128], P(('grp', 'leaf')), may hold values from -0.125 to 0.125
- coarse_points: float32 [8, 3, 128], replicated, may hold values from 0 to 1
Outputs:
- filtered: float32 [16, 524288], P(None, ('grp', 'leaf'))
The draws below stay inside these ranges and needn't reach their ends.
Inputs may be any that keep to these rules, and one draw needn't show every extreme that they name: `near_lists`: place w of leaf l's window is leaf (l // 2 - 1) * 2 + w. Slot 0 holds the leaf itself (2 + l % 2); the next slots hold distinct places of other leaves of the same subtree; then -1 to the end of the row. `inter_lists`: distinct leaves of the leaf's own subtree, numbered from the subtree's first leaf, none in the leaf's window. `skeleton`: distinct places within the leaf.
All inputs are finite; a program needn't handle non-finite values.
Results may differ from the reference program's by a relative error of at most 0.00013.
Values sent between devices are 32-bit elements; how exact they have to be, the bound alone decides.
A program may use at most 64 MiB of HBM per device.

```python
import math
import jax
import jax.numpy as jnp
from jax import lax

P_SIZE = 512
R = 64
RC = 128
VEC = 16
NB = 6
ILEN = 16
LEAF_DEV = 2
LEAVES_SUB = 128
LEAVES = 1024
POINTS = 524288
GROUPS = 8


def draw_points(key, part):
    leaf_ids = jnp.arange(LEAVES, dtype=jnp.int32)

    def spread(offset):
        result = jnp.zeros((LEAVES,), jnp.int32)
        for bit_pos in range(11):
            result = result + ((leaf_ids >> 3 * bit_pos + offset & 1) << bit_pos)
        return result.astype(jnp.float32)
    centres = jnp.stack([spread(0), spread(1), spread(2)]) * 0.08
    key_size, key_offset = jax.random.split(key)
    sizes = jnp.exp(jax.random.uniform(key_size, (LEAVES,), jnp.float32, math.log(1.5), math.log(3.0)))
    offsets = jax.random.uniform(key_offset, (3, LEAVES, P_SIZE), jnp.float32, -1.0, 1.0)
    coords = centres[:, :, None] + 0.04 * sizes[None, :, None] * offsets
    return coords.reshape(3, POINTS).astype(jnp.float32)


def draw_near_lists(key, part):
    width = 3 * LEAF_DEV
    leaf_ids = jnp.arange(LEAVES, dtype=jnp.int32)
    in_subtree = leaf_ids % LEAVES_SUB
    dev_place = in_subtree // LEAF_DEV
    own_place = in_subtree % LEAF_DEV
    places = jnp.arange(width, dtype=jnp.int32)
    target = (dev_place[:, None] - 1) * LEAF_DEV + places[None, :]
    usable = (target >= 0) & (target < LEAVES_SUB) & (places[None, :] != LEAF_DEV + own_place[:, None])
    key_score, key_dense, key_light = jax.random.split(key, 3)
    scores = jax.random.randint(key_score, (LEAVES, width), 0, 1 << 16) * (4 * width) + places[None, :]
    scores = scores + jnp.where(usable, 0, 1 << 28)
    order = jnp.argsort(scores, axis=1, stable=True)[:, :NB - 1].astype(jnp.int32)
    usable_count = jnp.sum(usable.astype(jnp.int32), axis=1)
    dense = jax.random.randint(key_dense, (LEAVES // LEAF_DEV,), 0, 4) == 0
    light = jax.random.randint(key_light, (LEAVES,), 0, NB // 2 + 1)
    others = jnp.where(dense[leaf_ids // LEAF_DEV], NB - 1, light)
    others = jnp.where(in_subtree == LEAF_DEV, NB - 1, others)
    others = jnp.minimum(others, usable_count)
    slots = jnp.arange(NB - 1, dtype=jnp.int32)
    rest = jnp.where(slots[None, :] < others[:, None], order, -1)
    return jnp.concatenate([(LEAF_DEV + own_place)[:, None], rest], axis=1).astype(jnp.int32)


def draw_inter_lists(key, part):
    leaf_ids = jnp.arange(LEAVES, dtype=jnp.int32)
    dev_place = leaf_ids % LEAVES_SUB // LEAF_DEV
    candidates = jnp.arange(LEAVES_SUB, dtype=jnp.int32)
    inside = (candidates[None, :] >= (dev_place[:, None] - 1) * LEAF_DEV) & (candidates[None, :] < (dev_place[:, None] + 2) * LEAF_DEV)
    scores = jax.random.randint(key, (LEAVES, LEAVES_SUB), 0, 1 << 16) * LEAVES_SUB + candidates[None, :]
    scores = scores + jnp.where(inside, 1 << 28, 0)
    return jnp.argsort(scores, axis=1, stable=True)[:, :ILEN].astype(jnp.int32)


def draw_skeleton(key, part):
    places = jnp.arange(P_SIZE, dtype=jnp.int32)
    scores = jax.random.randint(key, (LEAVES, P_SIZE), 0, 1 << 16) * P_SIZE + places[None, :]
    return jnp.argsort(scores, axis=1, stable=True)[:, :R].astype(jnp.int32)


def shard_levels(own_key, shape, shards, least, high):
    gain = 1.0
    for dim, parts in shards:
        steps = jax.random.uniform(jax.random.fold_in(jax.random.fold_in(own_key, 6), dim), (parts,), jnp.float32, least / len(shards), high / len(shards))
        gain = gain * jnp.repeat(jnp.exp(steps), shape[dim] // parts).reshape((-1,) + (1,) * (len(shape) - 1 - dim))
    return gain


def normal_values(own_key, extent, deviation, most, cuts=(), held_as=jnp.bfloat16):
    factor_of = shard_levels(own_key, extent, cuts, -0.22, 0.18) if cuts else 1.0
    array = jax.random.normal(own_key, extent, jnp.float32) * deviation * factor_of
    return jnp.minimum(jnp.maximum(array, -most), most).astype(held_as)


def setup_inputs(seed: int = 0) -> dict:
    arg_keys = jax.random.split(jax.random.key(seed), 9)
    return {
        "vectors": normal_values(arg_keys[0], (VEC, POINTS), 1.0, 6.0, ((1, 512),), jnp.float32),
        "points": draw_points(jax.random.fold_in(arg_keys[8], 71), 0),
        "near_lists": draw_near_lists(jax.random.fold_in(arg_keys[8], 71), 0),
        "inter_lists": draw_inter_lists(jax.random.fold_in(arg_keys[8], 71), 0),
        "skeleton": draw_skeleton(jax.random.fold_in(arg_keys[8], 71), 0),
        "interp": normal_values(arg_keys[5], (LEAVES, R, P_SIZE), P_SIZE ** -0.5, 0.25, ((0, 512),), jnp.float32),
        "transfer": normal_values(arg_keys[6], (LEAVES, R, RC), (32 * R) ** -0.5, 0.125, ((0, 512),), jnp.float32),
        "coarse_points": jnp.clip(jax.random.uniform(arg_keys[7], (GROUPS, 3, RC), jnp.float32, 0.0, 1.0), 0.0, 1.0),
    }


kappa_scale = 3.4641016151377544
centre = 0.05
half_width = 0.05
highest = lax.Precision.HIGHEST

def matern(source, target):
    delta_x = source[..., 0, :, None] - target[..., 0, None, :]
    delta_y = source[..., 1, :, None] - target[..., 1, None, :]
    delta_z = source[..., 2, :, None] - target[..., 2, None, :]
    scaled = kappa_scale * jnp.sqrt(delta_x * delta_x + delta_y * delta_y + delta_z * delta_z)
    return (1.0 + scaled) * jnp.exp(-scaled)

def operate(field, leaf_points, near_lists, inter_lists, skeleton, interp, transfer, coarse_points):
    leaf_vecs = field.reshape(VEC, LEAVES, P_SIZE).transpose(1, 0, 2)
    leaf_ids = jnp.arange(LEAVES, dtype=jnp.int32)
    base_leaf = (leaf_ids // LEAF_DEV - 1) * LEAF_DEV
    is_valid = near_lists >= 0
    near_global = jnp.where(is_valid, base_leaf[:, None] + near_lists, leaf_ids[:, None]).astype(jnp.int32)

    def near_one(leaf_id):
        sources = near_global[leaf_id]
        kernel = matern(leaf_points[sources], leaf_points[leaf_id])
        kernel = kernel * is_valid[leaf_id].astype(jnp.float32)[:, None, None]
        return jnp.einsum('kvp,kpq->vq', leaf_vecs[sources], kernel, precision=highest)
    near_part = lax.map(near_one, leaf_ids)
    coeffs = jnp.einsum('lvp,lrp->lvr', leaf_vecs, interp, precision=highest)
    skel_points = jnp.take_along_axis(leaf_points, skeleton[:, None, :], axis=2)
    list_global = ((leaf_ids // LEAVES_SUB * LEAVES_SUB)[:, None] + inter_lists).astype(jnp.int32)

    def far_one(leaf_id):
        sources = list_global[leaf_id]
        kernel = matern(skel_points[sources], skel_points[leaf_id])
        return jnp.einsum('svr,srq->vq', coeffs[sources], kernel, precision=highest)
    leaf_far = lax.map(far_one, leaf_ids)
    upward = jnp.einsum('lvr,lrc->lvc', coeffs, transfer, precision=highest)
    group_coeffs = upward.reshape(GROUPS, LEAVES_SUB, VEC, RC).sum(axis=1)
    coupling = matern(coarse_points[:, None], coarse_points[None, :])
    apart = (jnp.arange(GROUPS)[:, None] != jnp.arange(GROUPS)[None, :]).astype(jnp.float32)
    coarse_field = jnp.einsum('avr,agrq->gvq', group_coeffs, coupling * apart[:, :, None, None], precision=highest)
    leaf_coarse = coarse_field[leaf_ids // LEAVES_SUB]
    downward = leaf_far + jnp.einsum('lvc,lrc->lvr', leaf_coarse, transfer, precision=highest)
    far_part = jnp.einsum('lvr,lrp->lvp', downward, interp, precision=highest)
    total = (near_part + far_part) / (P_SIZE * NB)
    return total.transpose(1, 0, 2).reshape(VEC, POINTS)

def reference(vectors, points, near_lists, inter_lists, skeleton, interp, transfer, coarse_points):
    leaf_points = points.reshape(3, LEAVES, P_SIZE).transpose(1, 0, 2)

    def apply_once(field):
        return operate(field, leaf_points, near_lists, inter_lists, skeleton, interp, transfer, coarse_points)
    term_one = (apply_once(vectors) - centre * vectors) / half_width
    term_two = 2.0 * (apply_once(term_one) - centre * term_one) / half_width - vectors
    term_three = 2.0 * (apply_once(term_two) - centre * term_two) / half_width - term_one
    squares = lax.optimization_barrier(jnp.sum(term_three * term_three, axis=1))
    return term_three / jnp.sqrt(squares / POINTS + 1e-06)[:, None]
```

```python
import jax
import jax.numpy as jnp
from jax import lax
from jax.experimental import pallas as pl
from jax.experimental.pallas import tpu as pltpu
from jax.sharding import PartitionSpec as P

MESH = pl.DeviceIdType.MESH
F32, BF16 = jnp.float32, jnp.bfloat16
LN2 = 0.6931471805599453
ALPHA = 3.4641016151377544 / LN2
FAR_AWAY = 65536.0
CENTRE = 0.05
HALF_WIDTH = 0.05
POINTS = 524288
SCALE = 3072.0
PTS, SRC, TGT, HALO, CO, PLANE, ZED, EX, FAR, NORM_P, NORM_Z = 0, 1, 2, 3, 6, 9, 12, 15, 18, 21, 22
SEMS = 23


def dot(a, b):
    return jnp.dot(a, b, preferred_element_type=F32)


def split2(v):
    hi = v.astype(BF16)
    return hi, (v - hi.astype(F32)).astype(BF16)


def stacked(v):
    hi = v.astype(BF16).astype(F32)
    return jnp.concatenate([hi, v - hi], axis=0).astype(BF16)


def dot3(v2, whi, wlo):
    a = dot(v2, whi)
    return a[:16] + a[16:] + dot(v2[:16], wlo)


def split3(v):
    h = v.astype(BF16).astype(F32)
    m = (v - h).astype(BF16).astype(F32)
    return h, m, v - h - m


def norm_rows(q):
    h, m, lo = split3(jnp.sum(q * q, axis=0, keepdims=True))
    row = lax.broadcasted_iota(jnp.int32, q.shape, 0)
    parts = jnp.where(row == 0, h, jnp.where(row == 1, m, jnp.where(row == 2, lo, 0.0)))
    return parts, jnp.where(row < 3, 1.0, 0.0)


def source_features(q, mask_rows):
    h, m, lo = split3(q)
    parts, ones = norm_rows(q)
    pad = jnp.zeros((64 - mask_rows.shape[0], q.shape[1]), F32)
    return jnp.concatenate(
        [-2.0 * h, -2.0 * h, -2.0 * m, -2.0 * m, -2.0 * h, -2.0 * lo, parts, ones, mask_rows, pad], axis=0
    )


def target_features(q, mask_rows):
    h, m, lo = split3(q)
    parts, ones = norm_rows(q)
    pad = jnp.zeros((64 - mask_rows.shape[0], q.shape[1]), F32)
    return jnp.concatenate([h, m, h, m, lo, h, ones, parts, mask_rows, pad], axis=0).astype(BF16)


def matern(d):
    t = jnp.maximum(d, 1e-12)
    s = t * lax.rsqrt(t)
    return (1.0 + LN2 * s) * jnp.exp2(-s)


def kernel(
    vec_ref, pts_ref, near_ref, inter_ref, skel_ref, interp_ref, trans_ref, coarse_ref, out_ref,
    xs, xh, vh, ybuf, vcat, nacc, bhi, blo, bthi, btlo, tgt_near, src_f, khi, klo,
    s_send, s_recv, t_send, t_recv, tgt_far, fhi, flo, kc,
    usend, precv, wsend, zrecv, hsend, xrecv, csend, crecv, gsend, grecv,
    nsend, np_recv, nz_send, nz_recv, send_sem, recv_sem,
):
    g = lax.axis_index("grp")
    leaf = lax.axis_index("leaf")
    x, z = leaf // 16, leaf % 16
    zh, zl = z // 2, z % 2
    plane = g * 4 + x
    rho = x * 2 + zl

    def z_peer(k):
        return (g, x * 16 + lax.rem(z + k, 16))

    def plane_index(k):
        return lax.rem(plane + k, 32)

    def plane_peer(k):
        i = plane_index(k)
        return (i // 4, lax.rem(i, 4) * 16 + z)

    def x_peer(k):
        return (g, lax.rem(x + k, 4) * 16 + z)

    def r_peer(k):
        i = lax.rem(rho + k, 8)
        return (g, (i // 2) * 16 + zh * 2 + lax.rem(i, 2))

    def c_peer(k):
        return (g, x * 16 + lax.rem(zh + k, 8) * 2 + zl)

    right, left = (g, lax.rem(leaf + 1, 64)), (g, lax.rem(leaf + 63, 64))

    def send(src, dst, sem, peer):
        pltpu.make_async_remote_copy(
            src_ref=src, dst_ref=dst, send_sem=send_sem.at[sem], recv_sem=recv_sem.at[sem],
            device_id=peer, device_id_type=MESH,
        ).start()

    def arrived(ref, sem):
        pltpu.make_async_copy(ref, ref, recv_sem.at[sem]).wait()

    def sent(ref, sem):
        pltpu.make_async_copy(ref, ref, send_sem.at[sem]).wait()

    barrier = pltpu.get_barrier_semaphore()

    def greet(peer):
        pl.semaphore_signal(barrier, inc=1, device_id=peer, device_id_type=MESH)

    for k in range(1, 16):
        greet(z_peer(k))
    for k in range(1, 32):
        greet(plane_peer(k))
    for k in range(1, 8):
        greet(r_peer(k))
    greet(right)
    greet(left)

    xs[...] = jnp.zeros_like(xs)
    xs[0:3, :] = pts_ref[...]
    origin = xs[:, 0:1]

    for l in range(2):
        t_t = trans_ref[l].T
        e = jnp.dot(t_t, interp_ref[l], precision=lax.Precision.HIGHEST, preferred_element_type=F32)
        zero = jnp.zeros((64, 512), F32)
        lower = [interp_ref[l], zero] if l == 0 else [zero, interp_ref[l]]
        b = jnp.concatenate([e, *lower], axis=0)
        hi, lo = split2(b)
        bhi[:, l * 512 : (l + 1) * 512] = hi
        blo[:, l * 512 : (l + 1) * 512] = lo
        hi, lo = split2(b.T)
        bthi[l * 512 : (l + 1) * 512, :] = hi
        btlo[l * 512 : (l + 1) * 512, :] = lo

    both = []
    for l in range(2):
        pick = lax.broadcasted_iota(jnp.int32, (512, 64), 0) == skel_ref[l : l + 1, :]
        pick = jnp.where(pick, 1.0, 0.0).astype(BF16)
        h, m, lo = split3(xs[:, l * 512 : (l + 1) * 512])
        got = dot(jnp.concatenate([h, m, lo, jnp.zeros_like(h)], axis=0).astype(BF16), pick)
        both.append(got[0:8] + (got[8:16] + got[16:24]))
    skel = jnp.concatenate(both, axis=1)
    s_send[...] = skel
    s_recv[rho] = skel

    row = lax.broadcasted_iota(jnp.int32, (128, 128), 0)
    number = ((row >> 2) & 3) * 32 + (row >> 4) * 4 + (row & 3)
    first = lax.broadcasted_iota(jnp.int32, (1, 128), 1) < 64
    listed = jnp.zeros((128, 128), F32)
    for s in range(16):
        wanted = jnp.where(first, inter_ref[0, s], inter_ref[1, s])
        listed = jnp.where(number == wanted, 1.0, listed)
    off = (1.0 - listed) * FAR_AWAY
    for j in range(8):
        t_send[j, 0:8, :] = skel
        t_send[j, 8:24, :] = off[j * 16 : (j + 1) * 16]
    t_recv[zh] = t_send[zh]

    def split_field(y):
        vcat[:, 1024:2048] = stacked(y)

    def upward(i):
        uc = dot3(vcat[:, 1024:2048], bthi[...], btlo[...])
        for j in range(4):
            usend[i, j] = uc[4 * j : 4 * j + 4, 0:128]
        precv[i, plane] = usend[i, x]
        csend[i] = uc[:, 128:256]
        crecv[i, rho] = uc[:, 128:256]

    def send_plane(i):
        for k in range(1, 32):
            send(usend.at[i, lax.rem(plane_index(k), 4)], precv.at[i, plane], PLANE + i, plane_peer(k))

    def send_coeffs(i):
        for k in range(1, 8):
            send(csend.at[i], crecv.at[i, rho], CO + i, r_peer(k))

    def send_halo(i, field):
        send(field, vh.at[i, 0], HALO + i, right)
        send(field, vh.at[i, 1], HALO + i, left)

    def plane_to_z(i):
        arrived(precv.at[i, pl.ds(0, 31)], PLANE + i)
        cols = []
        for e in range(8):
            cols.append((precv[i, 4 * e] + precv[i, 4 * e + 1]) + (precv[i, 4 * e + 2] + precv[i, 4 * e + 3]))
        c4 = jnp.concatenate(cols, axis=1)
        hi = c4.astype(BF16).astype(F32)
        lhs = jnp.concatenate([hi, c4 - hi, jnp.zeros((8, 1024), F32)], axis=0).astype(BF16)
        r = dot(lhs, kc[...])
        w = r[0:4, 0:128] + r[4:8, 0:128] + r[0:4, 128:256]
        wsend[i] = w
        zrecv[i, z] = w
        for k in range(1, 16):
            send(wsend.at[i], zrecv.at[i, z], ZED + i, z_peer(k))

    def z_to_x(i):
        arrived(zrecv.at[i, pl.ds(0, 15)], ZED + i)
        h = jnp.sum(zrecv[i], axis=0)
        hsend[i] = h
        xrecv[i, x] = h
        for k in range(1, 4):
            send(hsend.at[i], xrecv.at[i, x], EX + i, x_peer(k))

    def far_partial(i):
        arrived(crecv.at[i, pl.ds(0, 7)], CO + i)
        c = jnp.concatenate([crecv[i, j] for j in range(8)], axis=1)
        part = dot3(stacked(c), fhi[...], flo[...])
        for j in range(8):
            gsend[i, j] = part[:, j * 128 : (j + 1) * 128]
        grecv[i, zh] = gsend[i, zh]
        for k in range(1, 8):
            send(gsend.at[i, lax.rem(zh + k, 8)], grecv.at[i, zh], FAR + i, c_peer(k))

    def near(lo, hi):
        return dot3(vcat[:, lo:hi], khi[lo:hi, :], klo[lo:hi, :])

    def take_halo(i):
        arrived(vh.at[i], HALO + i)
        vcat[:, 0:1024] = stacked(vh[i, 0])
        vcat[:, 2048:3072] = stacked(vh[i, 1])

    def downward(i):
        arrived(grecv.at[i, pl.ds(0, 7)], FAR + i)
        gq = jnp.sum(grecv[i], axis=0)
        arrived(xrecv.at[i, pl.ds(0, 3)], EX + i)
        h = jnp.concatenate([xrecv[i, j] for j in range(4)], axis=0)
        return (nacc[...] + dot3(stacked(jnp.concatenate([h, gq], axis=1)), bhi[...], blo[...])) / SCALE

    def local(v):
        return (v - origin) * ALPHA

    def near_features(points, first_place):
        r = lax.broadcasted_iota(jnp.int32, (8, 1024), 0)
        place = first_place + lax.broadcasted_iota(jnp.int32, (8, 1024), 1) // 512
        f = source_features(local(points), jnp.where(r == place, 1.0, 0.0))
        src_f[...] = f.T.astype(BF16)

    def near_kernel(base):
        def body(i, _):
            r = pl.multiple_of(i * 256, 256)
            for c in (0, 512):
                k = matern(dot(src_f[pl.ds(r, 256), :], tgt_near[:, c : c + 512]))
                hi, lo = split2(k)
                khi[pl.ds(base + r, 256), c : c + 512] = hi
                klo[pl.ds(base + r, 256), c : c + 512] = lo
            return 0

        lax.fori_loop(0, 4, body, 0)

    def far_kernel():
        half = lax.broadcasted_iota(jnp.int32, (16, 128), 1) // 64
        r = lax.broadcasted_iota(jnp.int32, (16, 128), 0)
        for j in range(8):
            f = source_features(local(s_recv[j]), jnp.where(r == 2 * j + half, 1.0, 0.0))
            src_f[j * 128 : (j + 1) * 128, :] = f.T.astype(BF16)
            tgt_far[:, j * 128 : (j + 1) * 128] = target_features(local(t_recv[j, 0:8, :]), t_recv[j, 8:24, :])

        def body(i, _):
            r = pl.multiple_of(i * 256, 256)
            for c in (0, 512):
                k = matern(dot(src_f[pl.ds(r, 256), :], tgt_far[:, c : c + 512]))
                hi, lo = split2(k)
                fhi[pl.ds(r, 256), c : c + 512] = hi
                flo[pl.ds(r, 256), c : c + 512] = lo
            return 0

        lax.fori_loop(0, 4, body, 0)

    def coarse_kernel():
        none = jnp.zeros((8, 128), F32)
        pad = jnp.zeros((5, 128), F32)
        own = (jnp.concatenate([coarse_ref[g], pad], axis=0) - 0.5) * ALPHA
        tgt = target_features(own, none)
        for e in range(8):
            q = (jnp.concatenate([coarse_ref[e], pad], axis=0) - 0.5) * ALPHA
            k = matern(dot(source_features(q, none).T.astype(BF16), tgt))
            k = k * jnp.where(g == e, 0.0, 1.0)
            hi, lo = split2(k)
            kc[e * 128 : (e + 1) * 128, 0:128] = hi
            kc[e * 128 : (e + 1) * 128, 128:256] = lo

    split_field(vec_ref[...])
    upward(0)

    pl.semaphore_wait(barrier, 15 + 31 + 7 + 2)

    send_plane(0)
    for k in range(1, 8):
        send(t_send.at[lax.rem(zh + k, 8)], t_recv.at[zh], TGT, c_peer(k))
    for k in range(1, 8):
        send(s_send, s_recv.at[rho], SRC, r_peer(k))
    send_coeffs(0)
    send(xs, xh.at[0], PTS, right)
    send(xs, xh.at[1], PTS, left)
    send_halo(0, vec_ref)

    coarse_kernel()
    r = lax.broadcasted_iota(jnp.int32, (8, 1024), 0)
    first = lax.broadcasted_iota(jnp.int32, (1, 1024), 1) < 512
    listed = jnp.zeros((8, 1024), F32)
    for s in range(6):
        listed = jnp.where(r == jnp.where(first, near_ref[0, s], near_ref[1, s]), 1.0, listed)
    tgt_near[...] = target_features(local(xs[...]), (1.0 - listed) * FAR_AWAY)
    near_features(xs[...], 2)
    near_kernel(1024)
    plane_to_z(0)
    nacc[...] = near(1024, 2048)
    arrived(s_recv.at[pl.ds(0, 7)], SRC)
    arrived(t_recv.at[pl.ds(0, 7)], TGT)
    far_kernel()
    far_partial(0)
    arrived(xh, PTS)
    near_features(xh[0], 0)
    near_kernel(0)
    z_to_x(0)
    near_features(xh[1], 4)
    near_kernel(2048)
    take_halo(0)
    nacc[...] += near(0, 1024) + near(2048, 3072)
    y = (downward(0) - CENTRE * vec_ref[...]) / HALF_WIDTH
    ybuf[0] = y

    for i in (1, 2):
        split_field(ybuf[i - 1])
        upward(i)
        send_plane(i)
        send_coeffs(i)
        send_halo(i, ybuf.at[i - 1])
        nacc[...] = near(1024, 2048)
        far_partial(i)
        plane_to_z(i)
        take_halo(i)
        nacc[...] += near(0, 1024) + near(2048, 3072)
        z_to_x(i)
        before = vec_ref[...] if i == 1 else ybuf[0]
        y = 2.0 * (downward(i) - CENTRE * ybuf[i - 1]) / HALF_WIDTH - before
        if i == 1:
            ybuf[1] = y

    lane = lax.broadcasted_iota(jnp.int32, (16, 128), 1)
    diagonal = lane == lax.broadcasted_iota(jnp.int32, (16, 128), 0)
    squares = jnp.sum(y * y, axis=1, keepdims=True)
    nsend[...] = jnp.sum(jnp.where(diagonal, squares, 0.0), axis=0, keepdims=True)
    np_recv[plane] = nsend[...]
    for k in range(1, 32):
        send(nsend, np_recv.at[plane], NORM_P, plane_peer(k))
    arrived(np_recv.at[pl.ds(0, 31)], NORM_P)
    nz_send[...] = jnp.sum(np_recv[...], axis=0)
    nz_recv[z] = nz_send[...]
    for k in range(1, 16):
        send(nz_send, nz_recv.at[z], NORM_Z, z_peer(k))
    arrived(nz_recv.at[pl.ds(0, 15)], NORM_Z)
    total = jnp.sum(nz_recv[...], axis=0)
    mean = jnp.sum(jnp.where(diagonal, total, 0.0), axis=1, keepdims=True) / POINTS
    out_ref[...] = y / jnp.sqrt(mean + 1e-06)

    sent(xh, PTS)
    sent(s_recv.at[pl.ds(0, 7)], SRC)
    sent(t_recv.at[pl.ds(0, 7)], TGT)
    for i in range(3):
        sent(precv.at[i, pl.ds(0, 31)], PLANE + i)
        sent(zrecv.at[i, pl.ds(0, 15)], ZED + i)
        sent(xrecv.at[i, pl.ds(0, 3)], EX + i)
        sent(crecv.at[i, pl.ds(0, 7)], CO + i)
        sent(grecv.at[i, pl.ds(0, 7)], FAR + i)
        sent(vh.at[i], HALO + i)
    sent(np_recv.at[pl.ds(0, 31)], NORM_P)
    sent(nz_recv.at[pl.ds(0, 15)], NORM_Z)


def on_device(vectors, points, near_lists, inter_lists, skeleton, interp, transfer, coarse_points):
    vmem = pl.BlockSpec(memory_space=pltpu.VMEM)
    smem = pl.BlockSpec(memory_space=pltpu.SMEM)
    V = pltpu.VMEM
    return pl.pallas_call(
        kernel,
        out_shape=jax.ShapeDtypeStruct((16, 1024), F32),
        in_specs=[vmem, vmem, smem, smem, vmem, vmem, vmem, vmem],
        out_specs=vmem,
        scratch_shapes=[
            V((8, 1024), F32),
            V((2, 8, 1024), F32),
            V((3, 2, 16, 1024), F32),
            V((2, 16, 1024), F32),
            V((32, 3072), BF16),
            V((16, 1024), F32),
            V((256, 1024), BF16),
            V((256, 1024), BF16),
            V((1024, 256), BF16),
            V((1024, 256), BF16),
            V((128, 1024), BF16),
            V((1024, 128), BF16),
            V((3072, 1024), BF16),
            V((3072, 1024), BF16),
            V((8, 128), F32),
            V((8, 8, 128), F32),
            V((8, 24, 128), F32),
            V((8, 24, 128), F32),
            V((128, 1024), BF16),
            V((1024, 1024), BF16),
            V((1024, 1024), BF16),
            V((1024, 256), BF16),
            V((3, 4, 4, 128), F32),
            V((3, 32, 4, 128), F32),
            V((3, 4, 128), F32),
            V((3, 16, 4, 128), F32),
            V((3, 4, 128), F32),
            V((3, 4, 4, 128), F32),
            V((3, 16, 128), F32),
            V((3, 8, 16, 128), F32),
            V((3, 8, 16, 128), F32),
            V((3, 8, 16, 128), F32),
            V((1, 128), F32),
            V((32, 1, 128), F32),
            V((1, 128), F32),
            V((16, 1, 128), F32),
            pltpu.SemaphoreType.DMA((SEMS,)),
            pltpu.SemaphoreType.DMA((SEMS,)),
        ],
        compiler_params=pltpu.CompilerParams(
            collective_id=0, has_side_effects=True, vmem_limit_bytes=56 * 2**20
        ),
        name="filter",
    )(vectors, points, near_lists, inter_lists, skeleton, interp, transfer, coarse_points)


def solution(mesh):
    both = ("grp", "leaf")
    return jax.shard_map(
        on_device,
        mesh=mesh,
        in_specs=(
            P(None, both), P(None, both), P(both, None), P(both, None), P(both, None),
            P(both, None, None), P(both, None, None), P(),
        ),
        out_specs=P(None, both),
        check_vma=False,
    )
```

```python
import jax
import jax.numpy as jnp
from jax import lax
from jax.experimental import pallas as pl
from jax.experimental.pallas import tpu as pltpu
from jax.sharding import PartitionSpec as P

MESH = pl.DeviceIdType.MESH
F32, BF16 = jnp.float32, jnp.bfloat16
LN2 = 0.6931471805599453
ALPHA = 3.4641016151377544 / LN2
FAR_AWAY = 65536.0
CENTRE = 0.05
HALF_WIDTH = 0.05
POINTS = 524288
SCALE = 3072.0
PTS, SRC, TGT, HALO, CO, PLANE, ZED, EX, FAR, NORM_P, NORM_Z = 0, 1, 2, 3, 6, 9, 12, 15, 18, 21, 22
GRAM_Z, GRAM_X, GRAM_ALL, MIX = 23, 24, 25, 26
SEMS = 27
Z_ORDER = (8, 7, 9, 6, 10, 5, 11, 4, 12, 3, 13, 2, 14, 1, 15)
C_ORDER = (4, 3, 5, 2, 6, 1, 7)
PLANE_ORDER = (18, 17, 19, 16, 14, 22, 15, 13, 21, 23, 12, 20, 10, 26, 9, 11, 25, 27, 8, 24, 2, 30, 6, 1, 3, 5, 7, 29, 31, 28, 4)


def dot(a, b):
    return jnp.dot(a, b, preferred_element_type=F32)


def dot_t(a, b):
    return lax.dot_general(a, b, (((1,), (1,)), ((), ())), preferred_element_type=F32)


def split2(v):
    hi = v.astype(BF16)
    return hi, (v - hi.astype(F32)).astype(BF16)


def stacked(v):
    hi = v.astype(BF16).astype(F32)
    return jnp.concatenate([hi, v - hi], axis=0).astype(BF16)


def dot3(v2, whi, wlo):
    a = dot(v2, whi)
    return a[:16] + a[16:] + dot(v2[:16], wlo)


def split3(v):
    h = v.astype(BF16).astype(F32)
    m = (v - h).astype(BF16).astype(F32)
    return h, m, v - h - m


def norm_rows(q):
    h, m, lo = split3(jnp.sum(q * q, axis=0, keepdims=True))
    row = lax.broadcasted_iota(jnp.int32, q.shape, 0)
    parts = jnp.where(row == 0, h, jnp.where(row == 1, m, jnp.where(row == 2, lo, 0.0)))
    return parts, jnp.where(row < 3, 1.0, 0.0)


def source_features(q, mask_rows):
    h, m, lo = split3(q)
    parts, ones = norm_rows(q)
    pad = jnp.zeros((64 - mask_rows.shape[0], q.shape[1]), F32)
    return jnp.concatenate(
        [-2.0 * h, -2.0 * h, -2.0 * m, -2.0 * m, -2.0 * h, -2.0 * lo, parts, ones, mask_rows, pad], axis=0
    )


def target_features(q, mask_rows):
    h, m, lo = split3(q)
    parts, ones = norm_rows(q)
    pad = jnp.zeros((64 - mask_rows.shape[0], q.shape[1]), F32)
    return jnp.concatenate([h, m, h, m, lo, h, ones, parts, mask_rows, pad], axis=0).astype(BF16)


def matern(d):
    t = jnp.maximum(d, 1e-12)
    s = t * lax.rsqrt(t)
    return (1.0 + LN2 * s) * jnp.exp2(-s)


def kernel(
    vec_in, pts_in, near_in, inter_in, skel_in, interp_in, trans_in, coarse_in, out_ref,
    vec_ref, pts_ref, near_ref, inter_ref, skel_ref, interp_ref, trans_ref, coarse_ref,
    xs, xh, vh, ybuf, vcat, nacc, bhi, blo, bthi, btlo, tgt_near, src_f, khi, klo,
    s_send, s_recv, t_send, t_recv, tgt_far, fhi, flo, kc,
    usend, precv, wsend, zrecv, hsend, xrecv, csend, crecv, gsend, grecv,
    nsend, np_recv, nz_send, nz_recv,
    ga_send, ga_recv, gb_send, gb_recv, gc_send, gc_recv, gram, gram2, mx_send, mx_recv, send_sem, recv_sem, in_sem,
):
    g = lax.axis_index("grp")
    leaf = lax.axis_index("leaf")
    x, z = leaf // 16, leaf % 16
    zh, zl = z // 2, z % 2
    plane = g * 4 + x
    rho = x * 2 + zl

    def z_peer(k):
        return (g, x * 16 + lax.rem(z + k, 16))

    def plane_index(k):
        return lax.rem(plane + k, 32)

    def plane_peer(k):
        i = plane_index(k)
        return (i // 4, lax.rem(i, 4) * 16 + z)

    def x_peer(k):
        return (g, lax.rem(x + k, 4) * 16 + z)

    def r_peer(k):
        i = lax.rem(rho + k, 8)
        return (g, (i // 2) * 16 + zh * 2 + lax.rem(i, 2))

    def c_peer(k):
        return (g, x * 16 + lax.rem(zh + k, 8) * 2 + zl)

    right, left = (g, lax.rem(leaf + 1, 64)), (g, lax.rem(leaf + 63, 64))

    def send(src, dst, sem, peer):
        pltpu.make_async_remote_copy(
            src_ref=src, dst_ref=dst, send_sem=send_sem.at[sem], recv_sem=recv_sem.at[sem],
            device_id=peer, device_id_type=MESH,
        ).start()

    def arrived(ref, sem):
        pltpu.make_async_copy(ref, ref, recv_sem.at[sem]).wait()

    def sent(ref, sem):
        pltpu.make_async_copy(ref, ref, send_sem.at[sem]).wait()

    loads = [
        pltpu.make_async_copy(src, dst, in_sem.at[n])
        for n, (src, dst) in enumerate((
            (vec_in, vec_ref), (interp_in, interp_ref), (trans_in, trans_ref), (pts_in, pts_ref),
            (skel_in, skel_ref), (near_in, near_ref), (inter_in, inter_ref), (coarse_in, coarse_ref),
        ))
    ]
    for load in loads:
        load.start()

    barrier = pltpu.get_barrier_semaphore()

    def greet(peer):
        pl.semaphore_signal(barrier, inc=1, device_id=peer, device_id_type=MESH)

    for k in range(1, 16):
        greet(z_peer(k))
    for k in range(1, 32):
        greet(plane_peer(k))
    for k in range(1, 8):
        greet(r_peer(k))
    greet(right)
    greet(left)

    for load in loads:
        load.wait()
    xs[...] = jnp.zeros_like(xs)
    xs[0:3, :] = pts_ref[...]
    origin = xs[:, 0:1]

    def bases():
        for l in range(2):
            t_t = trans_ref[l].T
            e = jnp.dot(t_t, interp_ref[l], precision=lax.Precision.HIGHEST, preferred_element_type=F32)
            zero = jnp.zeros((64, 512), F32)
            lower = [interp_ref[l], zero] if l == 0 else [zero, interp_ref[l]]
            b = jnp.concatenate([e, *lower], axis=0)
            hi, lo = split2(b)
            bhi[:, l * 512 : (l + 1) * 512] = hi
            blo[:, l * 512 : (l + 1) * 512] = lo
            hi, lo = split2(b.T)
            bthi[l * 512 : (l + 1) * 512, :] = hi
            btlo[l * 512 : (l + 1) * 512, :] = lo

    def skeletons():
        both = []
        for l in range(2):
            pick = lax.broadcasted_iota(jnp.int32, (512, 64), 0) == skel_ref[l : l + 1, :]
            pick = jnp.where(pick, 1.0, 0.0).astype(BF16)
            h, m, lo = split3(xs[:, l * 512 : (l + 1) * 512])
            got = dot(jnp.concatenate([h, m, lo, jnp.zeros_like(h)], axis=0).astype(BF16), pick)
            both.append(got[0:8] + (got[8:16] + got[16:24]))
        skel = jnp.concatenate(both, axis=1)
        s_send[...] = skel
        s_recv[rho] = skel

        row = lax.broadcasted_iota(jnp.int32, (128, 128), 0)
        number = ((row >> 2) & 3) * 32 + (row >> 4) * 4 + (row & 3)
        first = lax.broadcasted_iota(jnp.int32, (1, 128), 1) < 64
        listed = jnp.zeros((128, 128), F32)
        for s in range(16):
            wanted = jnp.where(first, inter_ref[0, s], inter_ref[1, s])
            listed = jnp.where(number == wanted, 1.0, listed)
        off = (1.0 - listed) * FAR_AWAY
        for j in range(8):
            t_send[j, 0:8, :] = skel
            t_send[j, 8:24, :] = off[j * 16 : (j + 1) * 16]
        t_recv[zh] = t_send[zh]

    def split_field(y):
        vcat[:, 1024:2048] = stacked(y)

    def keep_plane(i, u):
        for j in range(4):
            usend[i, j] = u[4 * j : 4 * j + 4]
        precv[i, plane] = usend[i, x]

    def keep_coeffs(i, c):
        csend[i] = c
        crecv[i, rho] = c

    def keep_upward(i, u, c):
        keep_plane(i, u)
        keep_coeffs(i, c)

    def upward(i):
        uc = dot3(vcat[:, 1024:2048], bthi[...], btlo[...])
        keep_upward(i, uc[:, 0:128], uc[:, 128:256])

    def exact(a, b, contract):
        return lax.dot_general(
            a, b, (((1,), (contract,)), ((), ())), precision=lax.Precision.HIGHEST, preferred_element_type=F32
        )

    def first_upward():
        c = [exact(vec_ref[:, l * 512 : (l + 1) * 512], interp_ref[l], 1) for l in range(2)]
        keep_upward(0, exact(c[0], trans_ref[0], 0) + exact(c[1], trans_ref[1], 0), jnp.concatenate(c, axis=1))

    def send_plane(i):
        for k in PLANE_ORDER:
            send(usend.at[i, lax.rem(plane_index(k), 4)], precv.at[i, plane], PLANE + i, plane_peer(k))

    def send_coeffs(i):
        for k in range(1, 8):
            send(csend.at[i], crecv.at[i, rho], CO + i, r_peer(k))

    def send_halo(i, field):
        send(field, vh.at[i, 0], HALO + i, right)
        send(field, vh.at[i, 1], HALO + i, left)

    def couple(c4, w2):
        hi = c4.astype(BF16).astype(F32)
        lhs = jnp.concatenate([hi, c4 - hi, jnp.zeros((8, c4.shape[1]), F32)], axis=0).astype(BF16)
        r = dot(lhs, w2[...])
        return r[0:4, 0:128] + r[4:8, 0:128] + r[0:4, 128:256]

    def plane_to_z(i):
        arrived(precv.at[i, pl.ds(0, 31)], PLANE + i)
        cols = []
        for e in range(8):
            cols.append((precv[i, 4 * e] + precv[i, 4 * e + 1]) + (precv[i, 4 * e + 2] + precv[i, 4 * e + 3]))
        w = couple(jnp.concatenate(cols, axis=1), kc)
        wsend[i] = w
        zrecv[i, z] = w
        for k in Z_ORDER:
            send(wsend.at[i], zrecv.at[i, z], ZED + i, z_peer(k))

    def z_to_x(i, more=0.0):
        arrived(zrecv.at[i, pl.ds(0, 15)], ZED + i)
        h = jnp.sum(zrecv[i], axis=0) + more
        hsend[i] = h
        xrecv[i, x] = h
        for k in range(1, 4):
            send(hsend.at[i], xrecv.at[i, x], EX + i, x_peer(k))

    def gram_own():
        e, f = bhi[0:128, :], blo[0:128, :]
        m = dot_t(e, e) + (dot_t(e, f) + dot_t(f, e))
        for j in range(16):
            ga_send[j] = m[j * 8 : (j + 1) * 8]
        ga_recv[z] = ga_send[z]
        for k in Z_ORDER:
            send(ga_send.at[lax.rem(z + k, 16)], ga_recv.at[z], GRAM_Z, z_peer(k))

    def gram_x():
        arrived(ga_recv.at[pl.ds(0, 15)], GRAM_Z)
        m = jnp.sum(ga_recv[...], axis=0)
        gb_send[...] = m
        gb_recv[x] = m
        for k in range(1, 4):
            send(gb_send, gb_recv.at[x], GRAM_X, x_peer(k))

    def gram_all():
        arrived(gb_recv.at[pl.ds(0, 3)], GRAM_X)
        m = jnp.sum(gb_recv[...], axis=0)
        gc_send[...] = m
        gc_recv[z] = m
        for k in Z_ORDER:
            send(gc_send, gc_recv.at[z], GRAM_ALL, z_peer(k))

    def mix_send():
        arrived(gc_recv.at[pl.ds(0, 15)], GRAM_ALL)
        for j in range(16):
            gram[j * 8 : (j + 1) * 8, :] = gc_recv[j]
        hi, lo = split2(gram[...])
        gram2[:, 0:128] = hi
        gram2[:, 128:256] = lo
        mx_send[...] = couple(hsend[1], gram2)
        mx_recv[g] = mx_send[...]
        for k in (4, 3, 5, 2, 6, 1, 7):
            send(mx_send, mx_recv.at[g], MIX, (lax.rem(g + k, 8), leaf))

    def mix():
        arrived(mx_recv.at[pl.ds(0, 7)], MIX)
        return couple(jnp.concatenate([mx_recv[e] for e in range(8)], axis=1), kc)

    def far_partial(i):
        arrived(crecv.at[i, pl.ds(0, 7)], CO + i)
        c = jnp.concatenate([crecv[i, j] for j in range(8)], axis=1)
        part = dot3(stacked(c), fhi[...], flo[...])
        for j in range(8):
            gsend[i, j] = part[:, j * 128 : (j + 1) * 128]
        grecv[i, zh] = gsend[i, zh]
        for k in C_ORDER:
            send(gsend.at[i, lax.rem(zh + k, 8)], grecv.at[i, zh], FAR + i, c_peer(k))

    def near(lo, hi):
        return dot3(vcat[:, lo:hi], khi[lo:hi, :], klo[lo:hi, :])

    def take_halo(i):
        arrived(vh.at[i], HALO + i)
        vcat[:, 0:1024] = stacked(vh[i, 0])
        vcat[:, 2048:3072] = stacked(vh[i, 1])

    def leaf_far(i):
        arrived(grecv.at[i, pl.ds(0, 7)], FAR + i)
        return jnp.sum(grecv[i], axis=0)

    def coarse_field(i):
        arrived(xrecv.at[i, pl.ds(0, 3)], EX + i)
        return jnp.concatenate([xrecv[i, j] for j in range(4)], axis=0)

    def downward(i):
        gq = leaf_far(i)
        h = coarse_field(i)
        return (nacc[...] + dot3(stacked(jnp.concatenate([h, gq], axis=1)), bhi[...], blo[...])) / SCALE

    def local(v):
        return (v - origin) * ALPHA

    def near_features(points, first_place):
        r = lax.broadcasted_iota(jnp.int32, (8, 1024), 0)
        place = first_place + lax.broadcasted_iota(jnp.int32, (8, 1024), 1) // 512
        f = source_features(local(points), jnp.where(r == place, 1.0, 0.0))
        src_f[...] = f.T.astype(BF16)

    def near_kernel(base):
        def body(i, _):
            r = pl.multiple_of(i * 256, 256)
            for c in (0, 512):
                k = matern(dot(src_f[pl.ds(r, 256), :], tgt_near[:, c : c + 512]))
                hi, lo = split2(k)
                khi[pl.ds(base + r, 256), c : c + 512] = hi
                klo[pl.ds(base + r, 256), c : c + 512] = lo
            return 0

        lax.fori_loop(0, 4, body, 0)

    def far_kernel():
        half = lax.broadcasted_iota(jnp.int32, (16, 128), 1) // 64
        r = lax.broadcasted_iota(jnp.int32, (16, 128), 0)
        for j in range(8):
            f = source_features(local(s_recv[j]), jnp.where(r == 2 * j + half, 1.0, 0.0))
            src_f[j * 128 : (j + 1) * 128, :] = f.T.astype(BF16)
            tgt_far[:, j * 128 : (j + 1) * 128] = target_features(local(t_recv[j, 0:8, :]), t_recv[j, 8:24, :])

        def body(i, _):
            r = pl.multiple_of(i * 256, 256)
            for c in (0, 512):
                k = matern(dot(src_f[pl.ds(r, 256), :], tgt_far[:, c : c + 512]))
                hi, lo = split2(k)
                fhi[pl.ds(r, 256), c : c + 512] = hi
                flo[pl.ds(r, 256), c : c + 512] = lo
            return 0

        lax.fori_loop(0, 4, body, 0)

    def coarse_kernel():
        none = jnp.zeros((8, 128), F32)
        pad = jnp.zeros((5, 128), F32)
        own = (jnp.concatenate([coarse_ref[d, pl.ds(g, 1), :] for d in range(3)] + [pad], axis=0) - 0.5) * ALPHA
        tgt = target_features(own, none)
        for e in range(8):
            q = (jnp.concatenate([coarse_ref[d, e : e + 1, :] for d in range(3)] + [pad], axis=0) - 0.5) * ALPHA
            k = matern(dot(source_features(q, none).T.astype(BF16), tgt))
            k = k * jnp.where(g == e, 0.0, 1.0)
            hi, lo = split2(k)
            kc[e * 128 : (e + 1) * 128, 0:128] = hi
            kc[e * 128 : (e + 1) * 128, 128:256] = lo

    first_upward()

    pl.semaphore_wait(barrier, 15 + 31 + 7 + 2)

    send_plane(0)
    skeletons()
    for k in C_ORDER:
        send(t_send.at[lax.rem(zh + k, 8)], t_recv.at[zh], TGT, c_peer(k))
    for k in range(1, 8):
        send(s_send, s_recv.at[rho], SRC, r_peer(k))
    send_coeffs(0)
    send(xs, xh.at[0], PTS, right)
    send(xs, xh.at[1], PTS, left)
    send_halo(0, vec_ref)

    split_field(vec_ref[...])
    coarse_kernel()
    r = lax.broadcasted_iota(jnp.int32, (8, 1024), 0)
    first = lax.broadcasted_iota(jnp.int32, (1, 1024), 1) < 512
    listed = jnp.zeros((8, 1024), F32)
    for s in range(6):
        listed = jnp.where(r == jnp.where(first, near_ref[0, s], near_ref[1, s]), 1.0, listed)
    tgt_near[...] = target_features(local(xs[...]), (1.0 - listed) * FAR_AWAY)
    near_features(xs[...], 2)
    near_kernel(1024)
    plane_to_z(0)
    arrived(s_recv.at[pl.ds(0, 7)], SRC)
    arrived(t_recv.at[pl.ds(0, 7)], TGT)
    far_kernel()
    far_partial(0)
    bases()
    nacc[...] = near(1024, 2048)
    arrived(xh, PTS)
    near_features(xh[0], 0)
    near_kernel(0)
    z_to_x(0)
    near_features(xh[1], 4)
    near_kernel(2048)
    take_halo(0)
    nacc[...] += near(0, 1024) + near(2048, 3072)
    y = (downward(0) - CENTRE * vec_ref[...]) / HALF_WIDTH
    ybuf[0] = y

    gain = 2.0 / (HALF_WIDTH * SCALE)
    split_field(ybuf[0])
    upward(1)
    send_plane(1)
    send_coeffs(1)
    send_halo(1, ybuf.at[0])
    nacc[...] = near(1024, 2048)
    gram_own()
    far_partial(1)
    plane_to_z(1)
    take_halo(1)
    nacc[...] += near(0, 1024) + near(2048, 3072)
    gram_x()
    z_to_x(1)
    part = nacc[...] + dot3(stacked(leaf_far(1)), bhi[128:256, :], blo[128:256, :])
    part = gain * part - (2.0 * CENTRE / HALF_WIDTH) * ybuf[0] - vec_ref[...]
    keep_plane(2, dot3(stacked(part), bthi[:, 0:128], btlo[:, 0:128]))
    send_plane(2)
    gram_all()
    y = part + gain * dot3(stacked(coarse_field(1)), bhi[0:128, :], blo[0:128, :])
    ybuf[1] = y
    split_field(y)
    keep_coeffs(2, dot3(vcat[:, 1024:2048], bthi[:, 128:256], btlo[:, 128:256]))
    send_coeffs(2)
    send_halo(2, ybuf.at[1])
    nacc[...] = near(1024, 2048)
    plane_to_z(2)
    far_partial(2)
    mix_send()
    take_halo(2)
    nacc[...] += near(0, 1024) + near(2048, 3072)
    z_to_x(2, gain * mix())
    y = 2.0 * (downward(2) - CENTRE * ybuf[1]) / HALF_WIDTH - ybuf[0]

    lane = lax.broadcasted_iota(jnp.int32, (16, 128), 1)
    diagonal = lane == lax.broadcasted_iota(jnp.int32, (16, 128), 0)
    squares = jnp.sum(y * y, axis=1, keepdims=True)
    nsend[...] = jnp.sum(jnp.where(diagonal, squares, 0.0), axis=0, keepdims=True)
    np_recv[plane] = nsend[...]
    for k in PLANE_ORDER:
        send(nsend, np_recv.at[plane], NORM_P, plane_peer(k))
    sent(xh, PTS)
    sent(ga_recv.at[pl.ds(0, 15)], GRAM_Z)
    sent(gb_recv.at[pl.ds(0, 3)], GRAM_X)
    sent(gc_recv.at[pl.ds(0, 15)], GRAM_ALL)
    sent(mx_recv.at[pl.ds(0, 7)], MIX)
    sent(s_recv.at[pl.ds(0, 7)], SRC)
    sent(t_recv.at[pl.ds(0, 7)], TGT)
    for i in range(3):
        sent(precv.at[i, pl.ds(0, 31)], PLANE + i)
        sent(zrecv.at[i, pl.ds(0, 15)], ZED + i)
        sent(xrecv.at[i, pl.ds(0, 3)], EX + i)
        sent(crecv.at[i, pl.ds(0, 7)], CO + i)
        sent(grecv.at[i, pl.ds(0, 7)], FAR + i)
        sent(vh.at[i], HALO + i)
    arrived(np_recv.at[pl.ds(0, 31)], NORM_P)
    nz_send[...] = jnp.sum(np_recv[...], axis=0)
    nz_recv[z] = nz_send[...]
    for k in Z_ORDER:
        send(nz_send, nz_recv.at[z], NORM_Z, z_peer(k))
    arrived(nz_recv.at[pl.ds(0, 15)], NORM_Z)
    total = jnp.sum(nz_recv[...], axis=0)
    mean = jnp.sum(jnp.where(diagonal, total, 0.0), axis=1, keepdims=True) / POINTS
    out_ref[...] = y / jnp.sqrt(mean + 1e-06)

    sent(np_recv.at[pl.ds(0, 31)], NORM_P)
    sent(nz_recv.at[pl.ds(0, 15)], NORM_Z)


def on_device(vectors, points, near_lists, inter_lists, skeleton, interp, transfer, coarse_points):
    vmem = pl.BlockSpec(memory_space=pltpu.VMEM)
    V = pltpu.VMEM
    return pl.pallas_call(
        kernel,
        out_shape=jax.ShapeDtypeStruct((16, 1024), F32),
        in_specs=[pl.BlockSpec(memory_space=pl.ANY)] * 8,
        out_specs=vmem,
        scratch_shapes=[
            V((16, 1024), F32),
            V((3, 1024), F32),
            pltpu.SMEM((2, 6), jnp.int32),
            pltpu.SMEM((2, 16), jnp.int32),
            V((2, 64), jnp.int32),
            V((2, 64, 512), F32),
            V((2, 64, 128), F32),
            V((3, 8, 128), F32),
            V((8, 1024), F32),
            V((2, 8, 1024), F32),
            V((3, 2, 16, 1024), F32),
            V((2, 16, 1024), F32),
            V((32, 3072), BF16),
            V((16, 1024), F32),
            V((256, 1024), BF16),
            V((256, 1024), BF16),
            V((1024, 256), BF16),
            V((1024, 256), BF16),
            V((128, 1024), BF16),
            V((1024, 128), BF16),
            V((3072, 1024), BF16),
            V((3072, 1024), BF16),
            V((8, 128), F32),
            V((8, 8, 128), F32),
            V((8, 24, 128), F32),
            V((8, 24, 128), F32),
            V((128, 1024), BF16),
            V((1024, 1024), BF16),
            V((1024, 1024), BF16),
            V((1024, 256), BF16),
            V((3, 4, 4, 128), F32),
            V((3, 32, 4, 128), F32),
            V((3, 4, 128), F32),
            V((3, 16, 4, 128), F32),
            V((3, 4, 128), F32),
            V((3, 4, 4, 128), F32),
            V((3, 16, 128), F32),
            V((3, 8, 16, 128), F32),
            V((3, 8, 16, 128), F32),
            V((3, 8, 16, 128), F32),
            V((1, 128), F32),
            V((32, 1, 128), F32),
            V((1, 128), F32),
            V((16, 1, 128), F32),
            V((16, 8, 128), F32),
            V((16, 8, 128), F32),
            V((8, 128), F32),
            V((4, 8, 128), F32),
            V((8, 128), F32),
            V((16, 8, 128), F32),
            V((128, 128), F32),
            V((128, 256), BF16),
            V((4, 128), F32),
            V((8, 4, 128), F32),
            pltpu.SemaphoreType.DMA((SEMS,)),
            pltpu.SemaphoreType.DMA((SEMS,)),
            pltpu.SemaphoreType.DMA((8,)),
        ],
        compiler_params=pltpu.CompilerParams(
            collective_id=0, has_side_effects=True, vmem_limit_bytes=56 * 2**20
        ),
        name="filter",
    )(vectors, points, near_lists, inter_lists, skeleton, interp, transfer, coarse_points.transpose(1, 0, 2))


def solution(mesh):
    both = ("grp", "leaf")
    return jax.shard_map(
        on_device,
        mesh=mesh,
        in_specs=(
            P(None, both), P(None, both), P(both, None), P(both, None), P(both, None),
            P(both, None, None), P(both, None, None), P(),
        ),
        out_specs=P(None, both),
        check_vma=False,
    )
```

```python
import jax
import jax.numpy as jnp
from jax import lax
from jax.experimental import pallas as pl
from jax.experimental.pallas import tpu as pltpu
from jax.sharding import PartitionSpec as P

MESH = pl.DeviceIdType.MESH
F32, BF16 = jnp.float32, jnp.bfloat16
LN2 = 0.6931471805599453
ALPHA = 3.4641016151377544 / LN2
FAR_AWAY = 65536.0
CENTRE = 0.05
HALF_WIDTH = 0.05
POINTS = 524288
SCALE = 3072.0
PTS, SRC, TGT, HALO, CO, PLANE, ZED, EX, FAR, NORM_P, NORM_Z = 0, 1, 2, 3, 6, 9, 12, 15, 18, 21, 22
GRAM_Z, GRAM_X, GRAM_ALL, MIX = 23, 24, 25, 26
SEMS = 27
Z_ORDER = (8, 7, 9, 6, 10, 5, 11, 4, 12, 3, 13, 2, 14, 1, 15)
C_ORDER = (4, 3, 5, 2, 6, 1, 7)
PLANE_ORDER = (18, 17, 19, 16, 14, 22, 15, 13, 21, 23, 12, 20, 10, 26, 9, 11, 25, 27, 8, 24, 2, 30, 6, 1, 3, 5, 7, 29, 31, 28, 4)


def dot(a, b):
    return jnp.dot(a, b, preferred_element_type=F32)


def dot_t(a, b):
    return lax.dot_general(a, b, (((1,), (1,)), ((), ())), preferred_element_type=F32)


def split2(v):
    hi = v.astype(BF16)
    return hi, (v - hi.astype(F32)).astype(BF16)


def stacked(v):
    hi = v.astype(BF16).astype(F32)
    return jnp.concatenate([hi, v - hi], axis=0).astype(BF16)


def dot3(v2, whi, wlo):
    a = dot(v2, whi)
    return a[:16] + a[16:] + dot(v2[:16], wlo)


def split3(v):
    h = v.astype(BF16).astype(F32)
    m = (v - h).astype(BF16).astype(F32)
    return h, m, v - h - m


def norm_rows(q):
    h, m, lo = split3(jnp.sum(q * q, axis=0, keepdims=True))
    row = lax.broadcasted_iota(jnp.int32, q.shape, 0)
    parts = jnp.where(row == 0, h, jnp.where(row == 1, m, jnp.where(row == 2, lo, 0.0)))
    return parts, jnp.where(row < 3, 1.0, 0.0)


def source_features(q, mask_rows):
    h, m, lo = split3(q)
    parts, ones = norm_rows(q)
    pad = jnp.zeros((64 - mask_rows.shape[0], q.shape[1]), F32)
    return jnp.concatenate(
        [-2.0 * h, -2.0 * h, -2.0 * m, -2.0 * m, -2.0 * h, -2.0 * lo, parts, ones, mask_rows, pad], axis=0
    )


def target_features(q, mask_rows):
    h, m, lo = split3(q)
    parts, ones = norm_rows(q)
    pad = jnp.zeros((64 - mask_rows.shape[0], q.shape[1]), F32)
    return jnp.concatenate([h, m, h, m, lo, h, ones, parts, mask_rows, pad], axis=0).astype(BF16)


def matern(d):
    t = jnp.maximum(d, 1e-12)
    s = t * lax.rsqrt(t)
    return (1.0 + LN2 * s) * jnp.exp2(-s)


def kernel(
    vec_in, pts_in, near_in, inter_in, skel_in, interp_in, trans_in, coarse_in, out_ref,
    vec_ref, pts_ref, near_ref, inter_ref, skel_ref, interp_ref, trans_ref, coarse_ref,
    xs, xh, vh, ybuf, vcat, nacc, bhi, blo, bthi, btlo, tgt_near, src_f, far_f, khi, klo,
    s_send, s_recv, t_send, t_recv, tgt_far, fhi, flo, kc,
    usend, precv, wsend, zrecv, hsend, xrecv, csend, crecv, gsend, grecv,
    nsend, np_recv, nz_send, nz_recv,
    ga_send, ga_recv, gb_send, gb_recv, gc_send, gc_recv, gram, gram2, mx_send, mx_recv, send_sem, recv_sem, in_sem,
):
    g = lax.axis_index("grp")
    leaf = lax.axis_index("leaf")
    x, z = leaf // 16, leaf % 16
    zh, zl = z // 2, z % 2
    plane = g * 4 + x
    rho = x * 2 + zl

    def z_peer(k):
        return (g, x * 16 + lax.rem(z + k, 16))

    def plane_index(k):
        return lax.rem(plane + k, 32)

    def plane_peer(k):
        i = plane_index(k)
        return (i // 4, lax.rem(i, 4) * 16 + z)

    def x_peer(k):
        return (g, lax.rem(x + k, 4) * 16 + z)

    def r_peer(k):
        i = lax.rem(rho + k, 8)
        return (g, (i // 2) * 16 + zh * 2 + lax.rem(i, 2))

    def c_peer(k):
        return (g, x * 16 + lax.rem(zh + k, 8) * 2 + zl)

    right, left = (g, lax.rem(leaf + 1, 64)), (g, lax.rem(leaf + 63, 64))

    def send(src, dst, sem, peer):
        pltpu.make_async_remote_copy(
            src_ref=src, dst_ref=dst, send_sem=send_sem.at[sem], recv_sem=recv_sem.at[sem],
            device_id=peer, device_id_type=MESH,
        ).start()

    def arrived(ref, sem):
        pltpu.make_async_copy(ref, ref, recv_sem.at[sem]).wait()

    def sent(ref, sem):
        pltpu.make_async_copy(ref, ref, send_sem.at[sem]).wait()

    loads = [
        pltpu.make_async_copy(src, dst, in_sem.at[n])
        for n, (src, dst) in enumerate((
            (vec_in, vec_ref), (interp_in, interp_ref), (trans_in, trans_ref), (pts_in, pts_ref),
            (skel_in, skel_ref), (near_in, near_ref), (inter_in, inter_ref), (coarse_in, coarse_ref),
        ))
    ]
    for load in loads:
        load.start()

    barrier = pltpu.get_barrier_semaphore()

    def greet(peer):
        pl.semaphore_signal(barrier, inc=1, device_id=peer, device_id_type=MESH)

    for k in range(1, 16):
        greet(z_peer(k))
    for k in range(1, 32):
        greet(plane_peer(k))
    for k in range(1, 8):
        greet(r_peer(k))
    greet(right)
    greet(left)

    for load in loads:
        load.wait()
    xs[...] = jnp.zeros_like(xs)
    xs[0:3, :] = pts_ref[...]
    origin = xs[:, 0:1]

    def bases():
        for l in range(2):
            t_t = trans_ref[l].T
            e = jnp.dot(t_t, interp_ref[l], precision=lax.Precision.HIGHEST, preferred_element_type=F32)
            zero = jnp.zeros((64, 512), F32)
            lower = [interp_ref[l], zero] if l == 0 else [zero, interp_ref[l]]
            b = jnp.concatenate([e, *lower], axis=0)
            hi, lo = split2(b)
            bhi[:, l * 512 : (l + 1) * 512] = hi
            blo[:, l * 512 : (l + 1) * 512] = lo
            hi, lo = split2(b.T)
            bthi[l * 512 : (l + 1) * 512, :] = hi
            btlo[l * 512 : (l + 1) * 512, :] = lo

    def skeletons():
        both = []
        for l in range(2):
            pick = lax.broadcasted_iota(jnp.int32, (512, 64), 0) == skel_ref[l : l + 1, :]
            pick = jnp.where(pick, 1.0, 0.0).astype(BF16)
            h, m, lo = split3(xs[:, l * 512 : (l + 1) * 512])
            got = dot(jnp.concatenate([h, m, lo, jnp.zeros_like(h)], axis=0).astype(BF16), pick)
            both.append(got[0:8] + (got[8:16] + got[16:24]))
        skel = jnp.concatenate(both, axis=1)
        s_send[...] = skel
        s_recv[rho] = skel

        row = lax.broadcasted_iota(jnp.int32, (128, 128), 0)
        number = ((row >> 2) & 3) * 32 + (row >> 4) * 4 + (row & 3)
        first = lax.broadcasted_iota(jnp.int32, (1, 128), 1) < 64
        listed = jnp.zeros((128, 128), F32)
        for s in range(16):
            wanted = jnp.where(first, inter_ref[0, s], inter_ref[1, s])
            listed = jnp.where(number == wanted, 1.0, listed)
        off = (1.0 - listed) * FAR_AWAY
        for j in range(8):
            t_send[j, 0:8, :] = skel
            t_send[j, 8:24, :] = off[j * 16 : (j + 1) * 16]
        t_recv[zh] = t_send[zh]

    def split_field(y):
        vcat[:, 1024:2048] = stacked(y)

    def keep_plane(i, u):
        for j in range(4):
            usend[i, j] = u[4 * j : 4 * j + 4]
        precv[i, plane] = usend[i, x]

    def keep_coeffs(i, c):
        csend[i] = c
        crecv[i, rho] = c

    def keep_upward(i, u, c):
        keep_plane(i, u)
        keep_coeffs(i, c)

    def upward(i):
        uc = dot3(vcat[:, 1024:2048], bthi[...], btlo[...])
        keep_upward(i, uc[:, 0:128], uc[:, 128:256])

    def exact(a, b, contract):
        return lax.dot_general(
            a, b, (((1,), (contract,)), ((), ())), precision=lax.Precision.HIGHEST, preferred_element_type=F32
        )

    def first_upward():
        c = [exact(vec_ref[:, l * 512 : (l + 1) * 512], interp_ref[l], 1) for l in range(2)]
        keep_upward(0, exact(c[0], trans_ref[0], 0) + exact(c[1], trans_ref[1], 0), jnp.concatenate(c, axis=1))

    def send_plane(i):
        for k in PLANE_ORDER:
            send(usend.at[i, lax.rem(plane_index(k), 4)], precv.at[i, plane], PLANE + i, plane_peer(k))

    def send_coeffs(i):
        for k in range(1, 8):
            send(csend.at[i], crecv.at[i, rho], CO + i, r_peer(k))

    def send_halo(i, field):
        send(field, vh.at[i, 0], HALO + i, right)
        send(field, vh.at[i, 1], HALO + i, left)

    def couple(c4, w2):
        hi = c4.astype(BF16).astype(F32)
        lhs = jnp.concatenate([hi, c4 - hi, jnp.zeros((8, c4.shape[1]), F32)], axis=0).astype(BF16)
        r = dot(lhs, w2[...])
        return r[0:4, 0:128] + r[4:8, 0:128] + r[0:4, 128:256]

    def plane_to_z(i):
        arrived(precv.at[i, pl.ds(0, 31)], PLANE + i)
        cols = []
        for e in range(8):
            cols.append((precv[i, 4 * e] + precv[i, 4 * e + 1]) + (precv[i, 4 * e + 2] + precv[i, 4 * e + 3]))
        w = couple(jnp.concatenate(cols, axis=1), kc)
        wsend[i] = w
        zrecv[i, z] = w
        for k in Z_ORDER:
            send(wsend.at[i], zrecv.at[i, z], ZED + i, z_peer(k))

    def z_to_x(i, more=0.0):
        arrived(zrecv.at[i, pl.ds(0, 15)], ZED + i)
        h = jnp.sum(zrecv[i], axis=0) + more
        hsend[i] = h
        xrecv[i, x] = h
        for k in range(1, 4):
            send(hsend.at[i], xrecv.at[i, x], EX + i, x_peer(k))

    def gram_own():
        e, f = bhi[0:128, :], blo[0:128, :]
        m = dot_t(e, e) + (dot_t(e, f) + dot_t(f, e))
        for j in range(16):
            ga_send[j] = m[j * 8 : (j + 1) * 8]
        ga_recv[z] = ga_send[z]
        for k in Z_ORDER:
            send(ga_send.at[lax.rem(z + k, 16)], ga_recv.at[z], GRAM_Z, z_peer(k))

    def gram_x():
        arrived(ga_recv.at[pl.ds(0, 15)], GRAM_Z)
        m = jnp.sum(ga_recv[...], axis=0)
        gb_send[...] = m
        gb_recv[x] = m
        for k in range(1, 4):
            send(gb_send, gb_recv.at[x], GRAM_X, x_peer(k))

    def gram_all():
        arrived(gb_recv.at[pl.ds(0, 3)], GRAM_X)
        m = jnp.sum(gb_recv[...], axis=0)
        gc_send[...] = m
        gc_recv[z] = m
        for k in Z_ORDER:
            send(gc_send, gc_recv.at[z], GRAM_ALL, z_peer(k))

    def mix_send():
        arrived(gc_recv.at[pl.ds(0, 15)], GRAM_ALL)
        for j in range(16):
            gram[j * 8 : (j + 1) * 8, :] = gc_recv[j]
        hi, lo = split2(gram[...])
        gram2[:, 0:128] = hi
        gram2[:, 128:256] = lo
        mx_send[...] = couple(hsend[1], gram2)
        mx_recv[g] = mx_send[...]
        for k in (4, 3, 5, 2, 6, 1, 7):
            send(mx_send, mx_recv.at[g], MIX, (lax.rem(g + k, 8), leaf))

    def mix():
        arrived(mx_recv.at[pl.ds(0, 7)], MIX)
        return couple(jnp.concatenate([mx_recv[e] for e in range(8)], axis=1), kc)

    def far_partial(i):
        arrived(crecv.at[i, pl.ds(0, 7)], CO + i)
        c = jnp.concatenate([crecv[i, j] for j in range(8)], axis=1)
        part = dot3(stacked(c), fhi[...], flo[...])
        for j in range(8):
            gsend[i, j] = part[:, j * 128 : (j + 1) * 128]
        grecv[i, zh] = gsend[i, zh]
        for k in C_ORDER:
            send(gsend.at[i, lax.rem(zh + k, 8)], grecv.at[i, zh], FAR + i, c_peer(k))

    def near(lo, hi):
        return dot3(vcat[:, lo:hi], khi[lo:hi, :], klo[lo:hi, :])

    def take_halo(i):
        arrived(vh.at[i], HALO + i)
        vcat[:, 0:1024] = stacked(vh[i, 0])
        vcat[:, 2048:3072] = stacked(vh[i, 1])

    def leaf_far(i):
        arrived(grecv.at[i, pl.ds(0, 7)], FAR + i)
        return jnp.sum(grecv[i], axis=0)

    def coarse_field(i):
        arrived(xrecv.at[i, pl.ds(0, 3)], EX + i)
        return jnp.concatenate([xrecv[i, j] for j in range(4)], axis=0)

    def downward(i):
        gq = leaf_far(i)
        h = coarse_field(i)
        return (nacc[...] + dot3(stacked(jnp.concatenate([h, gq], axis=1)), bhi[...], blo[...])) / SCALE

    def local(v):
        return (v - origin) * ALPHA

    def near_features(points, first_place):
        r = lax.broadcasted_iota(jnp.int32, (8, 1024), 0)
        place = first_place + lax.broadcasted_iota(jnp.int32, (8, 1024), 1) // 512
        f = source_features(local(points), jnp.where(r == place, 1.0, 0.0))
        src_f[...] = f.T.astype(BF16)

    def near_kernel(base, first=0, last=2):
        def body(i, _):
            r = pl.multiple_of(i * 512, 512)
            for c in (0, 512):
                k = matern(dot(src_f[pl.ds(r, 512), :], tgt_near[:, c : c + 512]))
                hi, lo = split2(k)
                khi[pl.ds(base + r, 512), c : c + 512] = hi
                klo[pl.ds(base + r, 512), c : c + 512] = lo
            return 0

        lax.fori_loop(first, last, body, 0)

    def far_sources():
        half = lax.broadcasted_iota(jnp.int32, (16, 128), 1) // 64
        r = lax.broadcasted_iota(jnp.int32, (16, 128), 0)
        for j in range(8):
            f = source_features(local(s_recv[j]), jnp.where(r == 2 * j + half, 1.0, 0.0))
            far_f[j * 128 : (j + 1) * 128, :] = f.T.astype(BF16)

    def far_kernel():
        for j in range(8):
            tgt_far[:, j * 128 : (j + 1) * 128] = target_features(local(t_recv[j, 0:8, :]), t_recv[j, 8:24, :])

        def body(i, _):
            r = pl.multiple_of(i * 512, 512)
            for c in (0, 512):
                k = matern(dot(far_f[pl.ds(r, 512), :], tgt_far[:, c : c + 512]))
                hi, lo = split2(k)
                fhi[pl.ds(r, 512), c : c + 512] = hi
                flo[pl.ds(r, 512), c : c + 512] = lo
            return 0

        lax.fori_loop(0, 2, body, 0)

    def coarse_kernel():
        none = jnp.zeros((8, 128), F32)
        pad = jnp.zeros((5, 128), F32)
        own = (jnp.concatenate([coarse_ref[d, pl.ds(g, 1), :] for d in range(3)] + [pad], axis=0) - 0.5) * ALPHA
        tgt = target_features(own, none)
        for e in range(8):
            q = (jnp.concatenate([coarse_ref[d, e : e + 1, :] for d in range(3)] + [pad], axis=0) - 0.5) * ALPHA
            k = matern(dot(source_features(q, none).T.astype(BF16), tgt))
            k = k * jnp.where(g == e, 0.0, 1.0)
            hi, lo = split2(k)
            kc[e * 128 : (e + 1) * 128, 0:128] = hi
            kc[e * 128 : (e + 1) * 128, 128:256] = lo

    first_upward()
    skeletons()
    split_field(vec_ref[...])
    coarse_kernel()
    r = lax.broadcasted_iota(jnp.int32, (8, 1024), 0)
    first = lax.broadcasted_iota(jnp.int32, (1, 1024), 1) < 512
    listed = jnp.zeros((8, 1024), F32)
    for s in range(6):
        listed = jnp.where(r == jnp.where(first, near_ref[0, s], near_ref[1, s]), 1.0, listed)
    tgt_near[...] = target_features(local(xs[...]), (1.0 - listed) * FAR_AWAY)
    near_features(xs[...], 2)
    bases()
    near_kernel(1024, 0, 1)

    pl.semaphore_wait(barrier, 15 + 31 + 7 + 2)

    for k in C_ORDER:
        send(t_send.at[lax.rem(zh + k, 8)], t_recv.at[zh], TGT, c_peer(k))
    send_plane(0)
    for k in range(1, 8):
        send(s_send, s_recv.at[rho], SRC, r_peer(k))
    send_coeffs(0)
    send(xs, xh.at[0], PTS, right)
    send(xs, xh.at[1], PTS, left)
    send_halo(0, vec_ref)

    near_kernel(1024, 1, 2)
    arrived(s_recv.at[pl.ds(0, 7)], SRC)
    far_sources()
    plane_to_z(0)
    nacc[...] = near(1024, 2048)
    arrived(t_recv.at[pl.ds(0, 7)], TGT)
    far_kernel()
    far_partial(0)
    arrived(xh, PTS)
    near_features(xh[0], 0)
    near_kernel(0)
    z_to_x(0)
    near_features(xh[1], 4)
    near_kernel(2048)
    take_halo(0)
    nacc[...] += near(0, 1024) + near(2048, 3072)
    y = (downward(0) - CENTRE * vec_ref[...]) / HALF_WIDTH
    ybuf[0] = y

    gain = 2.0 / (HALF_WIDTH * SCALE)
    split_field(ybuf[0])
    upward(1)
    send_plane(1)
    send_coeffs(1)
    send_halo(1, ybuf.at[0])
    nacc[...] = near(1024, 2048)
    gram_own()
    far_partial(1)
    plane_to_z(1)
    take_halo(1)
    nacc[...] += near(0, 1024) + near(2048, 3072)
    gram_x()
    z_to_x(1)
    gram_all()
    part = nacc[...] + dot3(stacked(leaf_far(1)), bhi[128:256, :], blo[128:256, :])
    part = gain * part - (2.0 * CENTRE / HALF_WIDTH) * ybuf[0] - vec_ref[...]
    keep_plane(2, dot3(stacked(part), bthi[:, 0:128], btlo[:, 0:128]))
    send_plane(2)
    y = part + gain * dot3(stacked(coarse_field(1)), bhi[0:128, :], blo[0:128, :])
    ybuf[1] = y
    split_field(y)
    keep_coeffs(2, dot3(vcat[:, 1024:2048], bthi[:, 128:256], btlo[:, 128:256]))
    send_coeffs(2)
    send_halo(2, ybuf.at[1])
    nacc[...] = near(1024, 2048)
    mix_send()
    plane_to_z(2)
    far_partial(2)
    take_halo(2)
    nacc[...] += near(0, 1024) + near(2048, 3072)
    z_to_x(2, gain * mix())
    y = 2.0 * (downward(2) - CENTRE * ybuf[1]) / HALF_WIDTH - ybuf[0]

    lane = lax.broadcasted_iota(jnp.int32, (16, 128), 1)
    diagonal = lane == lax.broadcasted_iota(jnp.int32, (16, 128), 0)
    squares = jnp.sum(y * y, axis=1, keepdims=True)
    nsend[...] = jnp.sum(jnp.where(diagonal, squares, 0.0), axis=0, keepdims=True)
    np_recv[plane] = nsend[...]
    for k in PLANE_ORDER:
        send(nsend, np_recv.at[plane], NORM_P, plane_peer(k))
    sent(xh, PTS)
    sent(ga_recv.at[pl.ds(0, 15)], GRAM_Z)
    sent(gb_recv.at[pl.ds(0, 3)], GRAM_X)
    sent(gc_recv.at[pl.ds(0, 15)], GRAM_ALL)
    sent(mx_recv.at[pl.ds(0, 7)], MIX)
    sent(s_recv.at[pl.ds(0, 7)], SRC)
    sent(t_recv.at[pl.ds(0, 7)], TGT)
    for i in range(3):
        sent(precv.at[i, pl.ds(0, 31)], PLANE + i)
        sent(zrecv.at[i, pl.ds(0, 15)], ZED + i)
        sent(xrecv.at[i, pl.ds(0, 3)], EX + i)
        sent(crecv.at[i, pl.ds(0, 7)], CO + i)
        sent(grecv.at[i, pl.ds(0, 7)], FAR + i)
        sent(vh.at[i], HALO + i)
    arrived(np_recv.at[pl.ds(0, 31)], NORM_P)
    nz_send[...] = jnp.sum(np_recv[...], axis=0)
    nz_recv[z] = nz_send[...]
    for k in Z_ORDER:
        send(nz_send, nz_recv.at[z], NORM_Z, z_peer(k))
    arrived(nz_recv.at[pl.ds(0, 15)], NORM_Z)
    total = jnp.sum(nz_recv[...], axis=0)
    mean = jnp.sum(jnp.where(diagonal, total, 0.0), axis=1, keepdims=True) / POINTS
    out_ref[...] = y / jnp.sqrt(mean + 1e-06)

    sent(np_recv.at[pl.ds(0, 31)], NORM_P)
    sent(nz_recv.at[pl.ds(0, 15)], NORM_Z)


def on_device(vectors, points, near_lists, inter_lists, skeleton, interp, transfer, coarse_points):
    vmem = pl.BlockSpec(memory_space=pltpu.VMEM)
    V = pltpu.VMEM
    return pl.pallas_call(
        kernel,
        out_shape=jax.ShapeDtypeStruct((16, 1024), F32),
        in_specs=[pl.BlockSpec(memory_space=pl.ANY)] * 8,
        out_specs=vmem,
        scratch_shapes=[
            V((16, 1024), F32),
            V((3, 1024), F32),
            pltpu.SMEM((2, 6), jnp.int32),
            pltpu.SMEM((2, 16), jnp.int32),
            V((2, 64), jnp.int32),
            V((2, 64, 512), F32),
            V((2, 64, 128), F32),
            V((3, 8, 128), F32),
            V((8, 1024), F32),
            V((2, 8, 1024), F32),
            V((3, 2, 16, 1024), F32),
            V((2, 16, 1024), F32),
            V((32, 3072), BF16),
            V((16, 1024), F32),
            V((256, 1024), BF16),
            V((256, 1024), BF16),
            V((1024, 256), BF16),
            V((1024, 256), BF16),
            V((128, 1024), BF16),
            V((1024, 128), BF16),
            V((1024, 128), BF16),
            V((3072, 1024), BF16),
            V((3072, 1024), BF16),
            V((8, 128), F32),
            V((8, 8, 128), F32),
            V((8, 24, 128), F32),
            V((8, 24, 128), F32),
            V((128, 1024), BF16),
            V((1024, 1024), BF16),
            V((1024, 1024), BF16),
            V((1024, 256), BF16),
            V((3, 4, 4, 128), F32),
            V((3, 32, 4, 128), F32),
            V((3, 4, 128), F32),
            V((3, 16, 4, 128), F32),
            V((3, 4, 128), F32),
            V((3, 4, 4, 128), F32),
            V((3, 16, 128), F32),
            V((3, 8, 16, 128), F32),
            V((3, 8, 16, 128), F32),
            V((3, 8, 16, 128), F32),
            V((1, 128), F32),
            V((32, 1, 128), F32),
            V((1, 128), F32),
            V((16, 1, 128), F32),
            V((16, 8, 128), F32),
            V((16, 8, 128), F32),
            V((8, 128), F32),
            V((4, 8, 128), F32),
            V((8, 128), F32),
            V((16, 8, 128), F32),
            V((128, 128), F32),
            V((128, 256), BF16),
            V((4, 128), F32),
            V((8, 4, 128), F32),
            pltpu.SemaphoreType.DMA((SEMS,)),
            pltpu.SemaphoreType.DMA((SEMS,)),
            pltpu.SemaphoreType.DMA((8,)),
        ],
        compiler_params=pltpu.CompilerParams(
            collective_id=0, has_side_effects=True, vmem_limit_bytes=56 * 2**20
        ),
        name="filter",
    )(vectors, points, near_lists, inter_lists, skeleton, interp, transfer, coarse_points.transpose(1, 0, 2))


def solution(mesh):
    both = ("grp", "leaf")
    return jax.shard_map(
        on_device,
        mesh=mesh,
        in_specs=(
            P(None, both), P(None, both), P(both, None), P(both, None), P(both, None),
            P(both, None, None), P(both, None, None), P(),
        ),
        out_specs=P(None, both),
        check_vma=False,
    )
```

```python
import jax
import jax.numpy as jnp
from jax import lax
from jax.experimental import pallas as pl
from jax.experimental.pallas import tpu as pltpu
from jax.sharding import PartitionSpec as P

MESH = pl.DeviceIdType.MESH
F32, BF16 = jnp.float32, jnp.bfloat16
LN2 = 0.6931471805599453
ALPHA = 3.4641016151377544 / LN2
FAR_AWAY = 65536.0
CENTRE = 0.05
HALF_WIDTH = 0.05
POINTS = 524288
SCALE = 3072.0
PTS, SRC, TGT, HALO, CO, PLANE, ZED, EX, FAR, NORM_P, NORM_Z = 0, 1, 2, 3, 6, 9, 12, 15, 18, 21, 22
GRAM_Z, GRAM_X, GRAM_ALL, MIX = 23, 24, 25, 26
SEMS = 27
Z_ORDER = (8, 7, 9, 6, 10, 5, 11, 4, 12, 3, 13, 2, 14, 1, 15)
C_ORDER = (4, 3, 5, 2, 6, 1, 7)
PLANE_ORDER = (14, 18, 22, 6, 10, 13, 15, 17, 19, 21, 23, 26, 30, 2, 5, 7, 9, 11, 12, 16, 20, 25, 27, 29, 31, 1, 3, 4, 8, 24, 28)


def dot(a, b):
    return jnp.dot(a, b, preferred_element_type=F32)


def dot_t(a, b):
    return lax.dot_general(a, b, (((1,), (1,)), ((), ())), preferred_element_type=F32)


def split2(v):
    hi = v.astype(BF16)
    return hi, (v - hi.astype(F32)).astype(BF16)


def stacked(v):
    hi = v.astype(BF16).astype(F32)
    return jnp.concatenate([hi, v - hi], axis=0).astype(BF16)


def dot3(v2, whi, wlo):
    a = dot(v2, whi)
    return a[:16] + a[16:] + dot(v2[:16], wlo)


def split3(v):
    h = v.astype(BF16).astype(F32)
    m = (v - h).astype(BF16).astype(F32)
    return h, m, v - h - m


def norm_rows(q):
    h, m, lo = split3(jnp.sum(q * q, axis=0, keepdims=True))
    row = lax.broadcasted_iota(jnp.int32, q.shape, 0)
    parts = jnp.where(row == 0, h, jnp.where(row == 1, m, jnp.where(row == 2, lo, 0.0)))
    return parts, jnp.where(row < 3, 1.0, 0.0)


def source_features(q, mask_rows):
    h, m, lo = split3(q)
    parts, ones = norm_rows(q)
    pad = jnp.zeros((64 - mask_rows.shape[0], q.shape[1]), F32)
    return jnp.concatenate(
        [-2.0 * h, -2.0 * h, -2.0 * m, -2.0 * m, -2.0 * h, -2.0 * lo, parts, ones, mask_rows, pad], axis=0
    )


def target_features(q, mask_rows):
    h, m, lo = split3(q)
    parts, ones = norm_rows(q)
    pad = jnp.zeros((64 - mask_rows.shape[0], q.shape[1]), F32)
    return jnp.concatenate([h, m, h, m, lo, h, ones, parts, mask_rows, pad], axis=0).astype(BF16)


def matern(d):
    t = jnp.maximum(d, 1e-12)
    s = t * lax.rsqrt(t)
    return (1.0 + LN2 * s) * jnp.exp2(-s)


def kernel(
    vec_in, pts_in, near_in, inter_in, skel_in, interp_in, trans_in, coarse_in, out_ref,
    vec_ref, pts_ref, near_ref, inter_ref, skel_ref, interp_ref, trans_ref, coarse_ref,
    xs, xh, vh, ybuf, vcat, nacc, bhi, blo, bthi, btlo, tgt_near, src_f, far_f, khi, klo,
    s_send, s_recv, t_send, t_recv, tgt_far, fhi, flo, kc,
    usend, precv, wsend, zrecv, hsend, xrecv, csend, crecv, gsend, grecv,
    nsend, np_recv, nz_send, nz_recv,
    ga_send, ga_recv, gb_send, gb_recv, gc_send, gc_recv, gram, gram2, mx_send, mx_recv, send_sem, recv_sem, in_sem,
):
    g = lax.axis_index("grp")
    leaf = lax.axis_index("leaf")
    x, z = leaf // 16, leaf % 16
    zh, zl = z // 2, z % 2
    plane = g * 4 + x
    rho = x * 2 + zl

    groups = [lax.rem(g + k, 8) for k in range(8)]
    columns = [lax.rem(x + k, 4) for k in range(4)]
    leaves = [c * 16 + z for c in columns]
    levels = [lax.rem(z + k, 16) for k in range(16)]
    z_leaves = [x * 16 + n for n in levels]

    def z_peer(k):
        return (g, z_leaves[k])

    def plane_peer(k):
        return (groups[k // 4], leaves[k % 4])

    def x_peer(k):
        return (g, leaves[k])

    def r_peer(k):
        i = lax.rem(rho + k, 8)
        return (g, (i // 2) * 16 + zh * 2 + lax.rem(i, 2))

    def c_peer(k):
        return (g, x * 16 + lax.rem(zh + k, 8) * 2 + zl)

    right, left = (g, lax.rem(leaf + 1, 64)), (g, lax.rem(leaf + 63, 64))

    def send(src, dst, sem, peer):
        pltpu.make_async_remote_copy(
            src_ref=src, dst_ref=dst, send_sem=send_sem.at[sem], recv_sem=recv_sem.at[sem],
            device_id=peer, device_id_type=MESH,
        ).start()

    def arrived(ref, sem):
        pltpu.make_async_copy(ref, ref, recv_sem.at[sem]).wait()

    def sent(ref, sem):
        pltpu.make_async_copy(ref, ref, send_sem.at[sem]).wait()

    loads = [
        pltpu.make_async_copy(src, dst, in_sem.at[n])
        for n, (src, dst) in enumerate((
            (vec_in, vec_ref), (interp_in, interp_ref), (trans_in, trans_ref), (pts_in, pts_ref),
            (skel_in, skel_ref), (near_in, near_ref), (inter_in, inter_ref), (coarse_in, coarse_ref),
        ))
    ]
    for load in loads:
        load.start()

    barrier = pltpu.get_barrier_semaphore()

    def greet(peer):
        pl.semaphore_signal(barrier, inc=1, device_id=peer, device_id_type=MESH)

    for k in Z_ORDER:
        greet(z_peer(k))
    for k in PLANE_ORDER:
        greet(plane_peer(k))
    for k in range(1, 8):
        greet(r_peer(k))
    greet(right)
    greet(left)

    for load in loads:
        load.wait()
    xs[...] = jnp.zeros_like(xs)
    xs[0:3, :] = pts_ref[...]
    origin = xs[:, 0:1]

    def bases():
        for l in range(2):
            t_t = trans_ref[l].T
            e = jnp.dot(t_t, interp_ref[l], precision=lax.Precision.HIGHEST, preferred_element_type=F32)
            zero = jnp.zeros((64, 512), F32)
            lower = [interp_ref[l], zero] if l == 0 else [zero, interp_ref[l]]
            b = jnp.concatenate([e, *lower], axis=0)
            hi, lo = split2(b)
            bhi[:, l * 512 : (l + 1) * 512] = hi
            blo[:, l * 512 : (l + 1) * 512] = lo
            hi, lo = split2(b.T)
            bthi[l * 512 : (l + 1) * 512, :] = hi
            btlo[l * 512 : (l + 1) * 512, :] = lo

    def skeletons():
        both = []
        for l in range(2):
            pick = lax.broadcasted_iota(jnp.int32, (512, 64), 0) == skel_ref[l : l + 1, :]
            pick = jnp.where(pick, 1.0, 0.0).astype(BF16)
            h, m, lo = split3(xs[:, l * 512 : (l + 1) * 512])
            got = dot(jnp.concatenate([h, m, lo, jnp.zeros_like(h)], axis=0).astype(BF16), pick)
            both.append(got[0:8] + (got[8:16] + got[16:24]))
        skel = jnp.concatenate(both, axis=1)
        s_send[...] = skel
        s_recv[rho] = skel

        row = lax.broadcasted_iota(jnp.int32, (128, 128), 0)
        number = ((row >> 2) & 3) * 32 + (row >> 4) * 4 + (row & 3)
        first = lax.broadcasted_iota(jnp.int32, (1, 128), 1) < 64
        listed = jnp.zeros((128, 128), F32)
        for s in range(16):
            wanted = jnp.where(first, inter_ref[0, s], inter_ref[1, s])
            listed = jnp.where(number == wanted, 1.0, listed)
        off = (1.0 - listed) * FAR_AWAY
        for j in range(8):
            t_send[j, 0:8, :] = skel
            t_send[j, 8:24, :] = off[j * 16 : (j + 1) * 16]
        t_recv[zh] = t_send[zh]

    def split_field(y):
        vcat[:, 1024:2048] = stacked(y)

    def keep_plane(i, u):
        for j in range(4):
            usend[i, j] = u[4 * j : 4 * j + 4]
        precv[i, plane] = usend[i, x]

    def keep_coeffs(i, c):
        csend[i] = c
        crecv[i, rho] = c

    def keep_upward(i, u, c):
        keep_plane(i, u)
        keep_coeffs(i, c)

    def upward(i):
        uc = dot3(vcat[:, 1024:2048], bthi[...], btlo[...])
        keep_upward(i, uc[:, 0:128], uc[:, 128:256])

    def exact(a, b, contract):
        return lax.dot_general(
            a, b, (((1,), (contract,)), ((), ())), precision=lax.Precision.HIGHEST, preferred_element_type=F32
        )

    def first_upward():
        c = [exact(vec_ref[:, l * 512 : (l + 1) * 512], interp_ref[l], 1) for l in range(2)]
        keep_upward(0, exact(c[0], trans_ref[0], 0) + exact(c[1], trans_ref[1], 0), jnp.concatenate(c, axis=1))

    def send_plane(i):
        for k in PLANE_ORDER:
            send(usend.at[i, columns[k % 4]], precv.at[i, plane], PLANE + i, plane_peer(k))

    def send_coeffs(i):
        for k in range(1, 8):
            send(csend.at[i], crecv.at[i, rho], CO + i, r_peer(k))

    def send_halo(i, field):
        send(field, vh.at[i, 0], HALO + i, right)
        send(field, vh.at[i, 1], HALO + i, left)

    def couple(c4, w2):
        hi = c4.astype(BF16).astype(F32)
        lhs = jnp.concatenate([hi, c4 - hi, jnp.zeros((8, c4.shape[1]), F32)], axis=0).astype(BF16)
        r = dot(lhs, w2[...])
        return r[0:4, 0:128] + r[4:8, 0:128] + r[0:4, 128:256]

    def plane_to_z(i):
        arrived(precv.at[i, pl.ds(0, 31)], PLANE + i)
        cols = []
        for e in range(8):
            cols.append((precv[i, 4 * e] + precv[i, 4 * e + 1]) + (precv[i, 4 * e + 2] + precv[i, 4 * e + 3]))
        w = couple(jnp.concatenate(cols, axis=1), kc)
        wsend[i] = w
        zrecv[i, z] = w
        for k in Z_ORDER:
            send(wsend.at[i], zrecv.at[i, z], ZED + i, z_peer(k))

    def z_to_x(i, more=0.0):
        arrived(zrecv.at[i, pl.ds(0, 15)], ZED + i)
        h = jnp.sum(zrecv[i], axis=0) + more
        hsend[i] = h
        xrecv[i, x] = h
        for k in range(1, 4):
            send(hsend.at[i], xrecv.at[i, x], EX + i, x_peer(k))

    def gram_own():
        e, f = bhi[0:128, :], blo[0:128, :]
        m = dot_t(e, e) + (dot_t(e, f) + dot_t(f, e))
        for j in range(16):
            ga_send[j] = m[j * 8 : (j + 1) * 8]
        ga_recv[z] = ga_send[z]
        for k in Z_ORDER:
            send(ga_send.at[levels[k]], ga_recv.at[z], GRAM_Z, z_peer(k))

    def gram_x():
        arrived(ga_recv.at[pl.ds(0, 15)], GRAM_Z)
        m = jnp.sum(ga_recv[...], axis=0)
        gb_send[...] = m
        gb_recv[x] = m
        for k in range(1, 4):
            send(gb_send, gb_recv.at[x], GRAM_X, x_peer(k))

    def gram_all():
        arrived(gb_recv.at[pl.ds(0, 3)], GRAM_X)
        m = jnp.sum(gb_recv[...], axis=0)
        gc_send[...] = m
        gc_recv[z] = m
        for k in Z_ORDER:
            send(gc_send, gc_recv.at[z], GRAM_ALL, z_peer(k))

    def mix_send():
        arrived(gc_recv.at[pl.ds(0, 15)], GRAM_ALL)
        for j in range(16):
            gram[j * 8 : (j + 1) * 8, :] = gc_recv[j]
        hi, lo = split2(gram[...])
        gram2[:, 0:128] = hi
        gram2[:, 128:256] = lo
        mx_send[...] = couple(hsend[1], gram2)
        mx_recv[g] = mx_send[...]
        for k in (4, 3, 5, 2, 6, 1, 7):
            send(mx_send, mx_recv.at[g], MIX, (groups[k], leaf))

    def mix():
        arrived(mx_recv.at[pl.ds(0, 7)], MIX)
        return couple(jnp.concatenate([mx_recv[e] for e in range(8)], axis=1), kc)

    def far_partial(i):
        arrived(crecv.at[i, pl.ds(0, 7)], CO + i)
        c = jnp.concatenate([crecv[i, j] for j in range(8)], axis=1)
        part = dot3(stacked(c), fhi[...], flo[...])
        for j in range(8):
            gsend[i, j] = part[:, j * 128 : (j + 1) * 128]
        grecv[i, zh] = gsend[i, zh]
        for k in C_ORDER:
            send(gsend.at[i, lax.rem(zh + k, 8)], grecv.at[i, zh], FAR + i, c_peer(k))

    def near(lo, hi):
        return dot3(vcat[:, lo:hi], khi[lo:hi, :], klo[lo:hi, :])

    def take_halo(i):
        arrived(vh.at[i], HALO + i)
        vcat[:, 0:1024] = stacked(vh[i, 0])
        vcat[:, 2048:3072] = stacked(vh[i, 1])

    def leaf_far(i):
        arrived(grecv.at[i, pl.ds(0, 7)], FAR + i)
        return jnp.sum(grecv[i], axis=0)

    def coarse_field(i):
        arrived(xrecv.at[i, pl.ds(0, 3)], EX + i)
        return jnp.concatenate([xrecv[i, j] for j in range(4)], axis=0)

    def downward(i):
        gq = leaf_far(i)
        h = coarse_field(i)
        return (nacc[...] + dot3(stacked(jnp.concatenate([h, gq], axis=1)), bhi[...], blo[...])) / SCALE

    def local(v):
        return (v - origin) * ALPHA

    def near_features(points, first_place):
        r = lax.broadcasted_iota(jnp.int32, (8, 1024), 0)
        place = first_place + lax.broadcasted_iota(jnp.int32, (8, 1024), 1) // 512
        f = source_features(local(points), jnp.where(r == place, 1.0, 0.0))
        src_f[...] = f.T.astype(BF16)

    def near_kernel(base, first=0, last=2):
        def body(i, _):
            r = pl.multiple_of(i * 512, 512)
            for c in (0, 512):
                k = matern(dot(src_f[pl.ds(r, 512), :], tgt_near[:, c : c + 512]))
                hi, lo = split2(k)
                khi[pl.ds(base + r, 512), c : c + 512] = hi
                klo[pl.ds(base + r, 512), c : c + 512] = lo
            return 0

        lax.fori_loop(first, last, body, 0)

    def far_sources():
        half = lax.broadcasted_iota(jnp.int32, (16, 128), 1) // 64
        r = lax.broadcasted_iota(jnp.int32, (16, 128), 0)
        for j in range(8):
            f = source_features(local(s_recv[j]), jnp.where(r == 2 * j + half, 1.0, 0.0))
            far_f[j * 128 : (j + 1) * 128, :] = f.T.astype(BF16)

    def far_kernel():
        for j in range(8):
            tgt_far[:, j * 128 : (j + 1) * 128] = target_features(local(t_recv[j, 0:8, :]), t_recv[j, 8:24, :])

        def body(i, _):
            r = pl.multiple_of(i * 512, 512)
            for c in (0, 512):
                k = matern(dot(far_f[pl.ds(r, 512), :], tgt_far[:, c : c + 512]))
                hi, lo = split2(k)
                fhi[pl.ds(r, 512), c : c + 512] = hi
                flo[pl.ds(r, 512), c : c + 512] = lo
            return 0

        lax.fori_loop(0, 2, body, 0)

    def coarse_kernel():
        none = jnp.zeros((8, 128), F32)
        pad = jnp.zeros((5, 128), F32)
        own = (jnp.concatenate([coarse_ref[d, pl.ds(g, 1), :] for d in range(3)] + [pad], axis=0) - 0.5) * ALPHA
        tgt = target_features(own, none)
        for e in range(8):
            q = (jnp.concatenate([coarse_ref[d, e : e + 1, :] for d in range(3)] + [pad], axis=0) - 0.5) * ALPHA
            k = matern(dot(source_features(q, none).T.astype(BF16), tgt))
            k = k * jnp.where(g == e, 0.0, 1.0)
            hi, lo = split2(k)
            kc[e * 128 : (e + 1) * 128, 0:128] = hi
            kc[e * 128 : (e + 1) * 128, 128:256] = lo

    first_upward()
    skeletons()
    split_field(vec_ref[...])
    coarse_kernel()
    r = lax.broadcasted_iota(jnp.int32, (8, 1024), 0)
    first = lax.broadcasted_iota(jnp.int32, (1, 1024), 1) < 512
    listed = jnp.zeros((8, 1024), F32)
    for s in range(6):
        listed = jnp.where(r == jnp.where(first, near_ref[0, s], near_ref[1, s]), 1.0, listed)
    tgt_near[...] = target_features(local(xs[...]), (1.0 - listed) * FAR_AWAY)
    near_features(xs[...], 2)
    bases()
    near_kernel(1024, 0, 1)

    pl.semaphore_wait(barrier, 15 + 31 + 7 + 2)

    for k in C_ORDER:
        send(t_send.at[lax.rem(zh + k, 8)], t_recv.at[zh], TGT, c_peer(k))
    send_plane(0)
    for k in range(1, 8):
        send(s_send, s_recv.at[rho], SRC, r_peer(k))
    send_coeffs(0)
    send(xs, xh.at[0], PTS, right)
    send(xs, xh.at[1], PTS, left)
    send_halo(0, vec_ref)

    near_kernel(1024, 1, 2)
    arrived(s_recv.at[pl.ds(0, 7)], SRC)
    far_sources()
    plane_to_z(0)
    nacc[...] = near(1024, 2048)
    arrived(t_recv.at[pl.ds(0, 7)], TGT)
    far_kernel()
    far_partial(0)
    arrived(xh, PTS)
    near_features(xh[0], 0)
    near_kernel(0)
    z_to_x(0)
    near_features(xh[1], 4)
    near_kernel(2048)
    take_halo(0)
    nacc[...] += near(0, 1024) + near(2048, 3072)
    y = (downward(0) - CENTRE * vec_ref[...]) / HALF_WIDTH
    ybuf[0] = y

    gain = 2.0 / (HALF_WIDTH * SCALE)
    split_field(ybuf[0])
    upward(1)
    send_coeffs(1)
    send_plane(1)
    send_halo(1, ybuf.at[0])
    gram_own()
    far_partial(1)
    nacc[...] = near(1024, 2048)
    plane_to_z(1)
    take_halo(1)
    nacc[...] += near(0, 1024) + near(2048, 3072)
    gram_x()
    z_to_x(1)
    gram_all()
    part = nacc[...] + dot3(stacked(leaf_far(1)), bhi[128:256, :], blo[128:256, :])
    part = gain * part - (2.0 * CENTRE / HALF_WIDTH) * ybuf[0] - vec_ref[...]
    keep_plane(2, dot3(stacked(part), bthi[:, 0:128], btlo[:, 0:128]))
    send_plane(2)
    y = part + gain * dot3(stacked(coarse_field(1)), bhi[0:128, :], blo[0:128, :])
    ybuf[1] = y
    split_field(y)
    keep_coeffs(2, dot3(vcat[:, 1024:2048], bthi[:, 128:256], btlo[:, 128:256]))
    send_coeffs(2)
    send_halo(2, ybuf.at[1])
    nacc[...] = near(1024, 2048)
    plane_to_z(2)
    far_partial(2)
    mix_send()
    take_halo(2)
    nacc[...] += near(0, 1024) + near(2048, 3072)
    z_to_x(2, gain * mix())
    y = 2.0 * (downward(2) - CENTRE * ybuf[1]) / HALF_WIDTH - ybuf[0]

    lane = lax.broadcasted_iota(jnp.int32, (16, 128), 1)
    diagonal = lane == lax.broadcasted_iota(jnp.int32, (16, 128), 0)
    squares = jnp.sum(y * y, axis=1, keepdims=True)
    nsend[...] = jnp.sum(jnp.where(diagonal, squares, 0.0), axis=0, keepdims=True)
    np_recv[plane] = nsend[...]
    for k in PLANE_ORDER:
        send(nsend, np_recv.at[plane], NORM_P, plane_peer(k))
    sent(xh, PTS)
    sent(ga_recv.at[pl.ds(0, 15)], GRAM_Z)
    sent(gb_recv.at[pl.ds(0, 3)], GRAM_X)
    sent(gc_recv.at[pl.ds(0, 15)], GRAM_ALL)
    sent(mx_recv.at[pl.ds(0, 7)], MIX)
    sent(s_recv.at[pl.ds(0, 7)], SRC)
    sent(t_recv.at[pl.ds(0, 7)], TGT)
    for i in range(3):
        sent(precv.at[i, pl.ds(0, 31)], PLANE + i)
        sent(zrecv.at[i, pl.ds(0, 15)], ZED + i)
        sent(xrecv.at[i, pl.ds(0, 3)], EX + i)
        sent(crecv.at[i, pl.ds(0, 7)], CO + i)
        sent(grecv.at[i, pl.ds(0, 7)], FAR + i)
        sent(vh.at[i], HALO + i)
    arrived(np_recv.at[pl.ds(0, 31)], NORM_P)
    nz_send[...] = jnp.sum(np_recv[...], axis=0)
    nz_recv[z] = nz_send[...]
    for k in Z_ORDER:
        send(nz_send, nz_recv.at[z], NORM_Z, z_peer(k))
    arrived(nz_recv.at[pl.ds(0, 15)], NORM_Z)
    total = jnp.sum(nz_recv[...], axis=0)
    mean = jnp.sum(jnp.where(diagonal, total, 0.0), axis=1, keepdims=True) / POINTS
    out_ref[...] = y / jnp.sqrt(mean + 1e-06)

    sent(np_recv.at[pl.ds(0, 31)], NORM_P)
    sent(nz_recv.at[pl.ds(0, 15)], NORM_Z)


def on_device(vectors, points, near_lists, inter_lists, skeleton, interp, transfer, coarse_points):
    vmem = pl.BlockSpec(memory_space=pltpu.VMEM)
    V = pltpu.VMEM
    return pl.pallas_call(
        kernel,
        out_shape=jax.ShapeDtypeStruct((16, 1024), F32),
        in_specs=[pl.BlockSpec(memory_space=pl.ANY)] * 8,
        out_specs=vmem,
        scratch_shapes=[
            V((16, 1024), F32),
            V((3, 1024), F32),
            pltpu.SMEM((2, 6), jnp.int32),
            pltpu.SMEM((2, 16), jnp.int32),
            V((2, 64), jnp.int32),
            V((2, 64, 512), F32),
            V((2, 64, 128), F32),
            V((3, 8, 128), F32),
            V((8, 1024), F32),
            V((2, 8, 1024), F32),
            V((3, 2, 16, 1024), F32),
            V((2, 16, 1024), F32),
            V((32, 3072), BF16),
            V((16, 1024), F32),
            V((256, 1024), BF16),
            V((256, 1024), BF16),
            V((1024, 256), BF16),
            V((1024, 256), BF16),
            V((128, 1024), BF16),
            V((1024, 128), BF16),
            V((1024, 128), BF16),
            V((3072, 1024), BF16),
            V((3072, 1024), BF16),
            V((8, 128), F32),
            V((8, 8, 128), F32),
            V((8, 24, 128), F32),
            V((8, 24, 128), F32),
            V((128, 1024), BF16),
            V((1024, 1024), BF16),
            V((1024, 1024), BF16),
            V((1024, 256), BF16),
            V((3, 4, 4, 128), F32),
            V((3, 32, 4, 128), F32),
            V((3, 4, 128), F32),
            V((3, 16, 4, 128), F32),
            V((3, 4, 128), F32),
            V((3, 4, 4, 128), F32),
            V((3, 16, 128), F32),
            V((3, 8, 16, 128), F32),
            V((3, 8, 16, 128), F32),
            V((3, 8, 16, 128), F32),
            V((1, 128), F32),
            V((32, 1, 128), F32),
            V((1, 128), F32),
            V((16, 1, 128), F32),
            V((16, 8, 128), F32),
            V((16, 8, 128), F32),
            V((8, 128), F32),
            V((4, 8, 128), F32),
            V((8, 128), F32),
            V((16, 8, 128), F32),
            V((128, 128), F32),
            V((128, 256), BF16),
            V((4, 128), F32),
            V((8, 4, 128), F32),
            pltpu.SemaphoreType.DMA((SEMS,)),
            pltpu.SemaphoreType.DMA((SEMS,)),
            pltpu.SemaphoreType.DMA((8,)),
        ],
        compiler_params=pltpu.CompilerParams(
            collective_id=0, has_side_effects=True, vmem_limit_bytes=56 * 2**20
        ),
        name="filter",
    )(vectors, points, near_lists, inter_lists, skeleton, interp, transfer, coarse_points.transpose(1, 0, 2))


def solution(mesh):
    both = ("grp", "leaf")
    return jax.shard_map(
        on_device,
        mesh=mesh,
        in_specs=(
            P(None, both), P(None, both), P(both, None), P(both, None), P(both, None),
            P(both, None, None), P(both, None, None), P(),
        ),
        out_specs=P(None, both),
        check_vma=False,
    )
```

```python
import jax
import jax.numpy as jnp
from jax import lax
from jax.experimental import pallas as pl
from jax.experimental.pallas import tpu as pltpu
from jax.sharding import PartitionSpec as P

MESH = pl.DeviceIdType.MESH
F32, BF16 = jnp.float32, jnp.bfloat16
LN2 = 0.6931471805599453
ALPHA = 3.4641016151377544 / LN2
FAR_AWAY = 65536.0
CENTRE = 0.05
HALF_WIDTH = 0.05
POINTS = 524288
SCALE = 3072.0
PTS, SRC, TGT, HALO, CO, PLANE, ZED, EX, FAR, NORM_P, NORM_Z = 0, 1, 2, 3, 6, 9, 12, 15, 18, 21, 22
GRAM_Z, GRAM_X, GRAM_ALL, MIX = 23, 24, 25, 26
SEMS = 27
Z_ORDER = (8, 7, 9, 6, 10, 5, 11, 4, 12, 3, 13, 2, 14, 1, 15)
C_ORDER = (4, 3, 5, 2, 6, 1, 7)
PLANE_ORDER = (14, 18, 22, 6, 10, 13, 15, 17, 19, 21, 23, 26, 30, 2, 5, 7, 9, 11, 12, 16, 20, 25, 27, 29, 31, 1, 3, 4, 8, 24, 28)


def dot(a, b):
    return jnp.dot(a, b, preferred_element_type=F32)


def dot_t(a, b):
    return lax.dot_general(a, b, (((1,), (1,)), ((), ())), preferred_element_type=F32)


def split2(v):
    hi = v.astype(BF16)
    return hi, (v - hi.astype(F32)).astype(BF16)


def stacked(v):
    hi = v.astype(BF16).astype(F32)
    return jnp.concatenate([hi, v - hi], axis=0).astype(BF16)


def dot3(v2, whi, wlo):
    a = dot(v2, whi)
    return a[:16] + a[16:] + dot(v2[:16], wlo)


def split3(v):
    h = v.astype(BF16).astype(F32)
    m = (v - h).astype(BF16).astype(F32)
    return h, m, v - h - m


def norm_rows(q):
    h, m, lo = split3(jnp.sum(q * q, axis=0, keepdims=True))
    row = lax.broadcasted_iota(jnp.int32, q.shape, 0)
    parts = jnp.where(row == 0, h, jnp.where(row == 1, m, jnp.where(row == 2, lo, 0.0)))
    return parts, jnp.where(row < 3, 1.0, 0.0)


def source_features(q, mask_rows):
    h, m, lo = split3(q)
    parts, ones = norm_rows(q)
    pad = jnp.zeros((64 - mask_rows.shape[0], q.shape[1]), F32)
    return jnp.concatenate(
        [-2.0 * h, -2.0 * h, -2.0 * m, -2.0 * m, -2.0 * h, -2.0 * lo, parts, ones, mask_rows, pad], axis=0
    )


def target_features(q, mask_rows):
    h, m, lo = split3(q)
    parts, ones = norm_rows(q)
    pad = jnp.zeros((64 - mask_rows.shape[0], q.shape[1]), F32)
    return jnp.concatenate([h, m, h, m, lo, h, ones, parts, mask_rows, pad], axis=0).astype(BF16)


def matern(d):
    t = jnp.maximum(d, 1e-12)
    s = t * lax.rsqrt(t)
    return (1.0 + LN2 * s) * jnp.exp2(-s)


def kernel(
    vec_in, pts_in, near_in, inter_in, skel_in, interp_in, trans_in, coarse_in, out_ref,
    vec_ref, pts_ref, near_ref, inter_ref, skel_ref, interp_ref, trans_ref, coarse_ref,
    xs, xh, vh, ybuf, vcat, nacc, bhi, blo, bthi, btlo, tgt_near, src_f, far_f, khi, klo,
    s_send, s_recv, t_send, t_recv, tgt_far, fhi, flo, kc,
    usend, precv, wsend, zrecv, hsend, xrecv, csend, crecv, gsend, grecv,
    nsend, np_recv, nz_send, nz_recv,
    ga_send, ga_recv, gb_send, gb_recv, gc_send, gc_recv, gram, gram2, mx_send, mx_recv, send_sem, recv_sem, in_sem,
):
    g = lax.axis_index("grp")
    leaf = lax.axis_index("leaf")
    x, z = leaf // 16, leaf % 16
    zh, zl = z // 2, z % 2
    plane = g * 4 + x
    rho = x * 2 + zl

    groups = [lax.rem(g + k, 8) for k in range(8)]
    columns = [lax.rem(x + k, 4) for k in range(4)]
    leaves = [c * 16 + z for c in columns]
    levels = [lax.rem(z + k, 16) for k in range(16)]
    z_leaves = [x * 16 + n for n in levels]

    def z_peer(k):
        return (g, z_leaves[k])

    def plane_peer(k):
        return (groups[k // 4], leaves[k % 4])

    def x_peer(k):
        return (g, leaves[k])

    def r_peer(k):
        i = lax.rem(rho + k, 8)
        return (g, (i // 2) * 16 + zh * 2 + lax.rem(i, 2))

    def c_peer(k):
        return (g, x * 16 + lax.rem(zh + k, 8) * 2 + zl)

    right, left = (g, lax.rem(leaf + 1, 64)), (g, lax.rem(leaf + 63, 64))

    def send(src, dst, sem, peer):
        pltpu.make_async_remote_copy(
            src_ref=src, dst_ref=dst, send_sem=send_sem.at[sem], recv_sem=recv_sem.at[sem],
            device_id=peer, device_id_type=MESH,
        ).start()

    def arrived(ref, sem):
        pltpu.make_async_copy(ref, ref, recv_sem.at[sem]).wait()

    def sent(ref, sem):
        pltpu.make_async_copy(ref, ref, send_sem.at[sem]).wait()

    loads = [
        pltpu.make_async_copy(src, dst, in_sem.at[n])
        for n, (src, dst) in enumerate((
            (vec_in, vec_ref), (interp_in, interp_ref), (trans_in, trans_ref), (pts_in, pts_ref),
            (skel_in, skel_ref), (near_in, near_ref), (inter_in, inter_ref), (coarse_in, coarse_ref),
        ))
    ]
    for load in loads:
        load.start()

    barrier = pltpu.get_barrier_semaphore()

    def greet(peer):
        pl.semaphore_signal(barrier, inc=1, device_id=peer, device_id_type=MESH)

    for k in Z_ORDER:
        greet(z_peer(k))
    for k in PLANE_ORDER:
        greet(plane_peer(k))
    for k in range(1, 8):
        greet(r_peer(k))
    greet(right)
    greet(left)

    for load in loads:
        load.wait()
    xs[...] = jnp.zeros_like(xs)
    xs[0:3, :] = pts_ref[...]
    origin = xs[:, 0:1]

    def bases():
        for l in range(2):
            t_t = trans_ref[l].T
            e = jnp.dot(t_t, interp_ref[l], precision=lax.Precision.HIGHEST, preferred_element_type=F32)
            zero = jnp.zeros((64, 512), F32)
            lower = [interp_ref[l], zero] if l == 0 else [zero, interp_ref[l]]
            b = jnp.concatenate([e, *lower], axis=0)
            hi, lo = split2(b)
            bhi[:, l * 512 : (l + 1) * 512] = hi
            blo[:, l * 512 : (l + 1) * 512] = lo
            hi, lo = split2(b.T)
            bthi[l * 512 : (l + 1) * 512, :] = hi
            btlo[l * 512 : (l + 1) * 512, :] = lo

    def skeletons():
        both = []
        for l in range(2):
            pick = lax.broadcasted_iota(jnp.int32, (512, 64), 0) == skel_ref[l : l + 1, :]
            pick = jnp.where(pick, 1.0, 0.0).astype(BF16)
            h, m, lo = split3(xs[:, l * 512 : (l + 1) * 512])
            got = dot(jnp.concatenate([h, m, lo, jnp.zeros_like(h)], axis=0).astype(BF16), pick)
            both.append(got[0:8] + (got[8:16] + got[16:24]))
        skel = jnp.concatenate(both, axis=1)
        s_send[...] = skel
        s_recv[rho] = skel

        row = lax.broadcasted_iota(jnp.int32, (128, 128), 0)
        number = ((row >> 2) & 3) * 32 + (row >> 4) * 4 + (row & 3)
        first = lax.broadcasted_iota(jnp.int32, (1, 128), 1) < 64
        listed = jnp.zeros((128, 128), F32)
        for s in range(16):
            wanted = jnp.where(first, inter_ref[0, s], inter_ref[1, s])
            listed = jnp.where(number == wanted, 1.0, listed)
        off = (1.0 - listed) * FAR_AWAY
        for j in range(8):
            t_send[j, 0:8, :] = skel
            t_send[j, 8:24, :] = off[j * 16 : (j + 1) * 16]
        t_recv[zh] = t_send[zh]

    def split_field(y):
        vcat[:, 1024:2048] = stacked(y)

    def keep_plane(i, u):
        for j in range(4):
            usend[i, j] = u[4 * j : 4 * j + 4]
        precv[i, plane] = usend[i, x]

    def keep_coeffs(i, c):
        csend[i] = c
        crecv[i, rho] = c

    def keep_upward(i, u, c):
        keep_plane(i, u)
        keep_coeffs(i, c)

    def upward(i):
        uc = dot3(vcat[:, 1024:2048], bthi[...], btlo[...])
        keep_upward(i, uc[:, 0:128], uc[:, 128:256])

    def exact(a, b, contract):
        return lax.dot_general(
            a, b, (((1,), (contract,)), ((), ())), precision=lax.Precision.HIGHEST, preferred_element_type=F32
        )

    def first_upward():
        c = [exact(vec_ref[:, l * 512 : (l + 1) * 512], interp_ref[l], 1) for l in range(2)]
        keep_upward(0, exact(c[0], trans_ref[0], 0) + exact(c[1], trans_ref[1], 0), jnp.concatenate(c, axis=1))

    def send_plane(i):
        for k in PLANE_ORDER:
            send(usend.at[i, columns[k % 4]], precv.at[i, plane], PLANE + i, plane_peer(k))

    def send_coeffs(i):
        for k in range(1, 8):
            send(csend.at[i], crecv.at[i, rho], CO + i, r_peer(k))

    def send_halo(i, field):
        send(field, vh.at[i, 0], HALO + i, right)
        send(field, vh.at[i, 1], HALO + i, left)

    def couple(c4, w2):
        hi = c4.astype(BF16).astype(F32)
        lhs = jnp.concatenate([hi, c4 - hi, jnp.zeros((8, c4.shape[1]), F32)], axis=0).astype(BF16)
        r = dot(lhs, w2[...])
        return r[0:4, 0:128] + r[4:8, 0:128] + r[0:4, 128:256]

    def plane_to_z(i):
        arrived(precv.at[i, pl.ds(0, 31)], PLANE + i)
        cols = []
        for e in range(8):
            cols.append((precv[i, 4 * e] + precv[i, 4 * e + 1]) + (precv[i, 4 * e + 2] + precv[i, 4 * e + 3]))
        w = couple(jnp.concatenate(cols, axis=1), kc)
        wsend[i] = w
        zrecv[i, z] = w
        for k in Z_ORDER:
            send(wsend.at[i], zrecv.at[i, z], ZED + i, z_peer(k))

    def z_to_x(i, more=0.0):
        arrived(zrecv.at[i, pl.ds(0, 15)], ZED + i)
        h = jnp.sum(zrecv[i], axis=0) + more
        hsend[i] = h
        xrecv[i, x] = h
        for k in range(1, 4):
            send(hsend.at[i], xrecv.at[i, x], EX + i, x_peer(k))

    def gram_own():
        e, f = bhi[0:128, :], blo[0:128, :]
        m = dot_t(e, e) + (dot_t(e, f) + dot_t(f, e))
        for j in range(16):
            ga_send[j] = m[j * 8 : (j + 1) * 8]
        ga_recv[z] = ga_send[z]
        for k in Z_ORDER:
            send(ga_send.at[levels[k]], ga_recv.at[z], GRAM_Z, z_peer(k))

    def gram_x():
        arrived(ga_recv.at[pl.ds(0, 15)], GRAM_Z)
        m = jnp.sum(ga_recv[...], axis=0)
        gb_send[...] = m
        gb_recv[x] = m
        for k in range(1, 4):
            send(gb_send, gb_recv.at[x], GRAM_X, x_peer(k))

    def gram_all():
        arrived(gb_recv.at[pl.ds(0, 3)], GRAM_X)
        m = jnp.sum(gb_recv[...], axis=0)
        gc_send[...] = m
        gc_recv[z] = m
        for k in Z_ORDER:
            send(gc_send, gc_recv.at[z], GRAM_ALL, z_peer(k))

    def mix_send():
        arrived(gc_recv.at[pl.ds(0, 15)], GRAM_ALL)
        for j in range(16):
            gram[j * 8 : (j + 1) * 8, :] = gc_recv[j]
        hi, lo = split2(gram[...])
        gram2[:, 0:128] = hi
        gram2[:, 128:256] = lo
        mx_send[...] = couple(hsend[1], gram2)
        mx_recv[g] = mx_send[...]
        for k in (4, 3, 5, 2, 6, 1, 7):
            send(mx_send, mx_recv.at[g], MIX, (groups[k], leaf))

    def mix():
        arrived(mx_recv.at[pl.ds(0, 7)], MIX)
        return couple(jnp.concatenate([mx_recv[e] for e in range(8)], axis=1), kc)

    def far_partial(i):
        arrived(crecv.at[i, pl.ds(0, 7)], CO + i)
        c = jnp.concatenate([crecv[i, j] for j in range(8)], axis=1)
        part = dot3(stacked(c), fhi[...], flo[...])
        for j in range(8):
            gsend[i, j] = part[:, j * 128 : (j + 1) * 128]
        grecv[i, zh] = gsend[i, zh]
        for k in C_ORDER:
            send(gsend.at[i, lax.rem(zh + k, 8)], grecv.at[i, zh], FAR + i, c_peer(k))

    def near(lo, hi):
        return dot3(vcat[:, lo:hi], khi[lo:hi, :], klo[lo:hi, :])

    def take_halo(i):
        arrived(vh.at[i], HALO + i)
        vcat[:, 0:1024] = stacked(vh[i, 0])
        vcat[:, 2048:3072] = stacked(vh[i, 1])

    def leaf_far(i):
        arrived(grecv.at[i, pl.ds(0, 7)], FAR + i)
        return jnp.sum(grecv[i], axis=0)

    def coarse_field(i):
        arrived(xrecv.at[i, pl.ds(0, 3)], EX + i)
        return jnp.concatenate([xrecv[i, j] for j in range(4)], axis=0)

    def downward(i):
        gq = leaf_far(i)
        h = coarse_field(i)
        return (nacc[...] + dot3(stacked(jnp.concatenate([h, gq], axis=1)), bhi[...], blo[...])) / SCALE

    def local(v):
        return (v - origin) * ALPHA

    def near_features(points, first_place):
        r = lax.broadcasted_iota(jnp.int32, (8, 1024), 0)
        place = first_place + lax.broadcasted_iota(jnp.int32, (8, 1024), 1) // 512
        f = source_features(local(points), jnp.where(r == place, 1.0, 0.0))
        src_f[...] = f.T.astype(BF16)

    def near_kernel(base, first=0, last=2):
        def body(i, _):
            r = pl.multiple_of(i * 512, 512)
            for c in (0, 512):
                k = matern(dot(src_f[pl.ds(r, 512), :], tgt_near[:, c : c + 512]))
                hi, lo = split2(k)
                khi[pl.ds(base + r, 512), c : c + 512] = hi
                klo[pl.ds(base + r, 512), c : c + 512] = lo
            return 0

        lax.fori_loop(first, last, body, 0)

    def far_sources():
        half = lax.broadcasted_iota(jnp.int32, (16, 128), 1) // 64
        r = lax.broadcasted_iota(jnp.int32, (16, 128), 0)
        for j in range(8):
            f = source_features(local(s_recv[j]), jnp.where(r == 2 * j + half, 1.0, 0.0))
            far_f[j * 128 : (j + 1) * 128, :] = f.T.astype(BF16)

    def far_kernel():
        for j in range(8):
            tgt_far[:, j * 128 : (j + 1) * 128] = target_features(local(t_recv[j, 0:8, :]), t_recv[j, 8:24, :])

        def body(i, _):
            r = pl.multiple_of(i * 512, 512)
            for c in (0, 512):
                k = matern(dot(far_f[pl.ds(r, 512), :], tgt_far[:, c : c + 512]))
                hi, lo = split2(k)
                fhi[pl.ds(r, 512), c : c + 512] = hi
                flo[pl.ds(r, 512), c : c + 512] = lo
            return 0

        lax.fori_loop(0, 2, body, 0)

    def coarse_kernel():
        none = jnp.zeros((8, 128), F32)
        pad = jnp.zeros((5, 128), F32)
        own = (jnp.concatenate([coarse_ref[d, pl.ds(g, 1), :] for d in range(3)] + [pad], axis=0) - 0.5) * ALPHA
        tgt = target_features(own, none)
        for e in range(8):
            q = (jnp.concatenate([coarse_ref[d, e : e + 1, :] for d in range(3)] + [pad], axis=0) - 0.5) * ALPHA
            k = matern(dot(source_features(q, none).T.astype(BF16), tgt))
            k = k * jnp.where(g == e, 0.0, 1.0)
            hi, lo = split2(k)
            kc[e * 128 : (e + 1) * 128, 0:128] = hi
            kc[e * 128 : (e + 1) * 128, 128:256] = lo

    first_upward()
    skeletons()
    split_field(vec_ref[...])
    coarse_kernel()
    r = lax.broadcasted_iota(jnp.int32, (8, 1024), 0)
    first = lax.broadcasted_iota(jnp.int32, (1, 1024), 1) < 512
    listed = jnp.zeros((8, 1024), F32)
    for s in range(6):
        listed = jnp.where(r == jnp.where(first, near_ref[0, s], near_ref[1, s]), 1.0, listed)
    tgt_near[...] = target_features(local(xs[...]), (1.0 - listed) * FAR_AWAY)
    near_features(xs[...], 2)
    bases()
    near_kernel(1024, 0, 1)

    pl.semaphore_wait(barrier, 15 + 31 + 7 + 2)

    for k in C_ORDER:
        send(t_send.at[lax.rem(zh + k, 8)], t_recv.at[zh], TGT, c_peer(k))
    send_plane(0)
    for k in range(1, 8):
        send(s_send, s_recv.at[rho], SRC, r_peer(k))
    send_coeffs(0)
    send(xs, xh.at[0], PTS, right)
    send(xs, xh.at[1], PTS, left)
    send_halo(0, vec_ref)

    near_kernel(1024, 1, 2)
    arrived(s_recv.at[pl.ds(0, 7)], SRC)
    far_sources()
    plane_to_z(0)
    nacc[...] = near(1024, 2048)
    arrived(t_recv.at[pl.ds(0, 7)], TGT)
    far_kernel()
    far_partial(0)
    arrived(xh, PTS)
    near_features(xh[0], 0)
    near_kernel(0, 0, 1)
    z_to_x(0)
    near_kernel(0, 1, 2)
    near_features(xh[1], 4)
    near_kernel(2048)
    take_halo(0)
    nacc[...] += near(0, 1024) + near(2048, 3072)
    y = (downward(0) - CENTRE * vec_ref[...]) / HALF_WIDTH
    ybuf[0] = y

    gain = 2.0 / (HALF_WIDTH * SCALE)
    split_field(ybuf[0])
    upward(1)
    send_plane(1)
    send_coeffs(1)
    send_halo(1, ybuf.at[0])
    nacc[...] = near(1024, 2048)
    gram_own()
    far_partial(1)
    plane_to_z(1)
    take_halo(1)
    nacc[...] += near(0, 1024) + near(2048, 3072)
    gram_x()
    z_to_x(1)
    gram_all()
    part = nacc[...] + dot3(stacked(leaf_far(1)), bhi[128:256, :], blo[128:256, :])
    part = gain * part - (2.0 * CENTRE / HALF_WIDTH) * ybuf[0] - vec_ref[...]
    keep_plane(2, dot3(stacked(part), bthi[:, 0:128], btlo[:, 0:128]))
    send_plane(2)
    y = part + gain * dot3(stacked(coarse_field(1)), bhi[0:128, :], blo[0:128, :])
    ybuf[1] = y
    split_field(y)
    keep_coeffs(2, dot3(vcat[:, 1024:2048], bthi[:, 128:256], btlo[:, 128:256]))
    send_coeffs(2)
    send_halo(2, ybuf.at[1])
    nacc[...] = near(1024, 2048)
    mix_send()
    plane_to_z(2)
    far_partial(2)
    take_halo(2)
    nacc[...] += near(0, 1024) + near(2048, 3072)
    z_to_x(2, gain * mix())
    y = 2.0 * (downward(2) - CENTRE * ybuf[1]) / HALF_WIDTH - ybuf[0]

    lane = lax.broadcasted_iota(jnp.int32, (16, 128), 1)
    diagonal = lane == lax.broadcasted_iota(jnp.int32, (16, 128), 0)
    squares = jnp.sum(y * y, axis=1, keepdims=True)
    nsend[...] = jnp.sum(jnp.where(diagonal, squares, 0.0), axis=0, keepdims=True)
    np_recv[plane] = nsend[...]
    for k in PLANE_ORDER:
        send(nsend, np_recv.at[plane], NORM_P, plane_peer(k))
    sent(xh, PTS)
    sent(ga_recv.at[pl.ds(0, 15)], GRAM_Z)
    sent(gb_recv.at[pl.ds(0, 3)], GRAM_X)
    sent(gc_recv.at[pl.ds(0, 15)], GRAM_ALL)
    sent(mx_recv.at[pl.ds(0, 7)], MIX)
    sent(s_recv.at[pl.ds(0, 7)], SRC)
    sent(t_recv.at[pl.ds(0, 7)], TGT)
    for i in range(3):
        sent(precv.at[i, pl.ds(0, 31)], PLANE + i)
        sent(zrecv.at[i, pl.ds(0, 15)], ZED + i)
        sent(xrecv.at[i, pl.ds(0, 3)], EX + i)
        sent(crecv.at[i, pl.ds(0, 7)], CO + i)
        sent(grecv.at[i, pl.ds(0, 7)], FAR + i)
        sent(vh.at[i], HALO + i)
    arrived(np_recv.at[pl.ds(0, 31)], NORM_P)
    nz_send[...] = jnp.sum(np_recv[...], axis=0)
    nz_recv[z] = nz_send[...]
    for k in Z_ORDER:
        send(nz_send, nz_recv.at[z], NORM_Z, z_peer(k))
    arrived(nz_recv.at[pl.ds(0, 15)], NORM_Z)
    total = jnp.sum(nz_recv[...], axis=0)
    mean = jnp.sum(jnp.where(diagonal, total, 0.0), axis=1, keepdims=True) / POINTS
    out_ref[...] = y / jnp.sqrt(mean + 1e-06)

    sent(np_recv.at[pl.ds(0, 31)], NORM_P)
    sent(nz_recv.at[pl.ds(0, 15)], NORM_Z)


def on_device(vectors, points, near_lists, inter_lists, skeleton, interp, transfer, coarse_points):
    vmem = pl.BlockSpec(memory_space=pltpu.VMEM)
    V = pltpu.VMEM
    return pl.pallas_call(
        kernel,
        out_shape=jax.ShapeDtypeStruct((16, 1024), F32),
        in_specs=[pl.BlockSpec(memory_space=pl.ANY)] * 8,
        out_specs=vmem,
        scratch_shapes=[
            V((16, 1024), F32),
            V((3, 1024), F32),
            pltpu.SMEM((2, 6), jnp.int32),
            pltpu.SMEM((2, 16), jnp.int32),
            V((2, 64), jnp.int32),
            V((2, 64, 512), F32),
            V((2, 64, 128), F32),
            V((3, 8, 128), F32),
            V((8, 1024), F32),
            V((2, 8, 1024), F32),
            V((3, 2, 16, 1024), F32),
            V((2, 16, 1024), F32),
            V((32, 3072), BF16),
            V((16, 1024), F32),
            V((256, 1024), BF16),
            V((256, 1024), BF16),
            V((1024, 256), BF16),
            V((1024, 256), BF16),
            V((128, 1024), BF16),
            V((1024, 128), BF16),
            V((1024, 128), BF16),
            V((3072, 1024), BF16),
            V((3072, 1024), BF16),
            V((8, 128), F32),
            V((8, 8, 128), F32),
            V((8, 24, 128), F32),
            V((8, 24, 128), F32),
            V((128, 1024), BF16),
            V((1024, 1024), BF16),
            V((1024, 1024), BF16),
            V((1024, 256), BF16),
            V((3, 4, 4, 128), F32),
            V((3, 32, 4, 128), F32),
            V((3, 4, 128), F32),
            V((3, 16, 4, 128), F32),
            V((3, 4, 128), F32),
            V((3, 4, 4, 128), F32),
            V((3, 16, 128), F32),
            V((3, 8, 16, 128), F32),
            V((3, 8, 16, 128), F32),
            V((3, 8, 16, 128), F32),
            V((1, 128), F32),
            V((32, 1, 128), F32),
            V((1, 128), F32),
            V((16, 1, 128), F32),
            V((16, 8, 128), F32),
            V((16, 8, 128), F32),
            V((8, 128), F32),
            V((4, 8, 128), F32),
            V((8, 128), F32),
            V((16, 8, 128), F32),
            V((128, 128), F32),
            V((128, 256), BF16),
            V((4, 128), F32),
            V((8, 4, 128), F32),
            pltpu.SemaphoreType.DMA((SEMS,)),
            pltpu.SemaphoreType.DMA((SEMS,)),
            pltpu.SemaphoreType.DMA((8,)),
        ],
        compiler_params=pltpu.CompilerParams(
            collective_id=0, has_side_effects=True, vmem_limit_bytes=56 * 2**20
        ),
        name="filter",
    )(vectors, points, near_lists, inter_lists, skeleton, interp, transfer, coarse_points.transpose(1, 0, 2))


def solution(mesh):
    both = ("grp", "leaf")
    return jax.shard_map(
        on_device,
        mesh=mesh,
        in_specs=(
            P(None, both), P(None, both), P(both, None), P(both, None), P(both, None),
            P(both, None, None), P(both, None, None), P(),
        ),
        out_specs=P(None, both),
        check_vma=False,
    )
```
